32 devices in a mesh: row: 8 (over z, x), col: 4 (over y, core).
Axes of the slice: x: 2, y: 2, z: 4, core: 2. Of those that a mesh axis runs over, the one named last changes fastest.
Arguments:
- hidden_in: bfloat16 [6144, 5120], P('row', 'col'), may hold values from -6 to 6
- modulation: bfloat16 [24, 3, 5120], P(None, None, 'col'), may hold values from -3 to 3
- w_qkv: bfloat16 [5120, 12288], P('row', 'col'), may hold values from -0.078125 to 0.078125
- w_out: bfloat16 [4096, 5120], P('row', 'col'), may hold values from -0.09375 to 0.09375
- prefix_cache: bfloat16 [8, 256, 8192], P('row', None, 'col'), may hold values from -48 to 48
- req_group: int32 [24], replicated, may hold values from 0 to 3
- req_len: int32 [24], replicated, may hold values from 1 to 672, 6144 in all
- owner: int32 [4], replicated, may hold values from 0 to 7, as said below
Outputs:
- hidden_out: bfloat16 [6144, 5120], P('row', 'col')
- suffix_keys: bfloat16 [6144, 4096], P('row', 'col')
- suffix_values: bfloat16 [6144, 4096], P('row', 'col')
The draws below stay inside these ranges and needn't reach their ends.
Inputs may be any that keep to these rules, and one draw needn't show every extreme that they name: `owner`: the 4 slots are distinct; slot 0 and slot 8 - 1 always hold a group.
All inputs are finite; a program needn't handle non-finite values.
Results may differ from the reference program's by a relative error of at most 0.006.
Values may be sent and summed in bfloat16 or wider, within the bound.
No kernel may reach another device: no remote copies, remote signals or barrier semaphores. Data moves between devices by JAX's collectives and lax.ppermute only.
A program may use at most 192 MiB of HBM per device.

```python
import math
import jax
import jax.numpy as jnp
import numpy as np
from jax import lax

D = 5120
HEADS = 32
HD = 128
TOK_DEV = 768
PREFIX = 256
GROUPS = 4
REQS = 24
TOKENS = 6144
MOST_LEN = 672
N_ROW = 8


def draw_owner(key, part):
    middle = jax.random.permutation(key, jnp.arange(1, N_ROW - 1, dtype=jnp.int32))
    chosen = jnp.concatenate([jnp.array([0, N_ROW - 1], dtype=jnp.int32), middle[:GROUPS - 2]])
    return jax.random.permutation(jax.random.fold_in(key, 7), chosen).astype(jnp.int32)


def draw_prefix_cache(key, part):
    key_base = jax.random.fold_in(key, 11)
    layout = (N_ROW, PREFIX, HEADS, 2, HD)
    cache = jax.random.truncated_normal(key_base, -6.0, 6.0, layout, jnp.float32)
    return cache.reshape(N_ROW, PREFIX, 2 * HEADS * HD).astype(jnp.bfloat16)


def place_ends(values, rng, low, top_value):
    spot = [jax.random.randint(jax.random.fold_in(rng, axis), (), 0, length) for axis, length in enumerate(values.shape)]
    longest = values.shape.index(max(values.shape))
    neighbour = spot[:longest] + [(spot[longest] + 1) % values.shape[longest]] + spot[longest + 1:]
    return values.at[tuple(spot)].set(low).at[tuple(neighbour)].set(top_value)


def shard_levels(stream_key, shape, pieces, low, high):
    level, own = 1.0, jax.random.fold_in(stream_key, 6)
    for dim, blocks in pieces:
        heights = jnp.exp(jax.random.uniform(jax.random.fold_in(own, dim), (blocks,), jnp.float32, low / len(pieces), high / len(pieces)))
        level = level * jnp.repeat(heights, shape[dim] // blocks).reshape([-1 if axis == dim else 1 for axis in range(len(shape))])
    return level


def profile(number_of, total, reach, skew):
    weights = [(1 << 20) // math.isqrt(standing ** skew) + 1 for standing in range(2, number_of + 1)]
    surplus, given = total - reach - (number_of - 1), [1] * (number_of - 1)
    while surplus > 0:
        movable = [i for i in range(number_of - 1) if given[i] < reach]
        pool, budget = sum([weights[i] for i in movable]), surplus
        for i in movable:
            extra = min(reach - given[i], max(1, budget * weights[i] // pool), surplus)
            given[i] = given[i] + extra
            surplus = surplus - extra
    return np.array([reach] + given)


def ragged_sizes(own_key, number_of, total, bound, slope):
    if number_of == 2:
        one = jax.random.randint(own_key, (), max(1, total - bound), min(bound, total - 1) + 1)
        return jnp.stack([one, total - one])
    sizes = jnp.asarray(profile(number_of, total, bound, slope), jnp.int32)
    couples = (number_of - 1) // 2
    donor, taker = sizes[1:1 + 2 * couples:2], sizes[2:2 + 2 * couples:2]
    slack = jnp.minimum(donor - 1, bound - taker)
    shifted = jax.random.randint(jax.random.fold_in(own_key, 1), (couples,), 0, 1 << 20) % (slack + 1)
    sizes = sizes.at[1:1 + 2 * couples:2].set(donor - shifted).at[2:2 + 2 * couples:2].set(taker + shifted)
    return sizes[jax.random.permutation(jax.random.fold_in(own_key, 2), number_of)]


def gaussian(own_key, dims, spread, most, pieces=(), held_as=jnp.bfloat16):
    entries = jax.random.normal(own_key, dims, jnp.float32) * spread
    if len(pieces) > 0:
        entries = shard_levels(own_key, dims, pieces, -0.22, 0.18) * entries
    return jnp.clip(entries, min=-most, max=most).astype(held_as)


def setup_inputs(seed: int = 0) -> dict:
    splits = jax.random.split(jax.random.key(seed), 9)
    return {
        "hidden_in": gaussian(splits[0], (TOKENS, D), 1.0, 6.0, ((0, 8), (1, 4))),
        "modulation": gaussian(splits[1], (REQS, 3, D), 0.5, 3.0, ((2, 4),)),
        "w_qkv": gaussian(splits[2], (D, 3 * HEADS * HD), D ** -0.5, 0.078125, ((0, 8), (1, 4))),
        "w_out": gaussian(splits[3], (HEADS * HD, D), (HEADS * HD) ** -0.5, 0.09375, ((0, 8), (1, 4))),
        "prefix_cache": draw_prefix_cache(jax.random.fold_in(splits[8], 71), 0),
        "req_group": place_ends(jax.random.randint(splits[5], (REQS,), 0, GROUPS), jax.random.fold_in(splits[5], 1), 0, GROUPS - 1).astype(jnp.int32),
        "req_len": ragged_sizes(splits[6], REQS, TOKENS, MOST_LEN, 2).astype(jnp.int32),
        "owner": draw_owner(jax.random.fold_in(splits[8], 71), 0),
    }


def request_of(positions, req_len):
    starts = (jnp.cumsum(req_len) - req_len).astype(jnp.int32)
    inside = (starts[None, :] <= positions[:, None]).astype(jnp.int32)
    return (lax.optimization_barrier(jnp.sum(inside, axis=1)) - 1).astype(jnp.int32)

def reference(hidden_in, modulation, w_qkv, w_out, prefix_cache, req_group, req_len, owner):
    positions = jnp.arange(TOKENS, dtype=jnp.int32)
    request_id = request_of(positions, req_len)
    onehot = (request_id[:, None] == jnp.arange(REQS, dtype=jnp.int32)[None, :]).astype(jnp.bfloat16)
    per_token = jnp.dot(onehot, modulation.reshape(REQS, 3 * D), preferred_element_type=jnp.float32)
    shift_rows = per_token[:, :D]
    scale_rows = per_token[:, D:2 * D]
    gate_rows = per_token[:, 2 * D:]
    hidden_f = hidden_in.astype(jnp.float32)
    average = lax.optimization_barrier(jnp.mean(hidden_f, axis=1, keepdims=True))
    centred = hidden_f - average
    variance = lax.optimization_barrier(jnp.mean(centred * centred, axis=1, keepdims=True))
    modulated = (centred * lax.rsqrt(variance + 1e-06) * (1.0 + scale_rows) + shift_rows).astype(jnp.bfloat16)
    projected_qkv = jnp.dot(modulated, w_qkv, preferred_element_type=jnp.float32).astype(jnp.bfloat16)
    projected_qkv = projected_qkv.reshape(TOKENS, HEADS, 3, HD)
    queries = projected_qkv[:, :, 0]
    new_keys = projected_qkv[:, :, 1]
    new_values = projected_qkv[:, :, 2]
    token_group = req_group[request_id].astype(jnp.int32)
    slots = prefix_cache.reshape(N_ROW, PREFIX, HEADS, 2, HD)[owner]
    prefix_keys = slots[:, :, :, 0].reshape(GROUPS * PREFIX, HEADS, HD).astype(jnp.float32)
    prefix_values = slots[:, :, :, 1].reshape(GROUPS * PREFIX, HEADS, HD).astype(jnp.float32)
    prefix_group = jnp.repeat(jnp.arange(GROUPS, dtype=jnp.int32), PREFIX)
    zero_block = jnp.zeros((TOK_DEV, HEADS, HD), jnp.bfloat16)
    keys_padded = jnp.concatenate([zero_block, new_keys, zero_block], axis=0)
    values_padded = jnp.concatenate([zero_block, new_values, zero_block], axis=0)
    outside = jnp.full((TOK_DEV,), -1, jnp.int32)
    request_padded = jnp.concatenate([outside, request_id, outside], axis=0)
    factor = 1.0 / math.sqrt(HD)

    def block(index):
        first = (index * TOK_DEV).astype(jnp.int32)
        query_block = lax.dynamic_slice_in_dim(queries, first, TOK_DEV, 0).astype(jnp.float32)
        query_req = lax.dynamic_slice_in_dim(request_id, first, TOK_DEV, 0)
        query_grp = lax.dynamic_slice_in_dim(token_group, first, TOK_DEV, 0)
        near_keys = lax.dynamic_slice_in_dim(keys_padded, first, 3 * TOK_DEV, 0).astype(jnp.float32)
        near_values = lax.dynamic_slice_in_dim(values_padded, first, 3 * TOK_DEV, 0).astype(jnp.float32)
        key_req = lax.dynamic_slice_in_dim(request_padded, first, 3 * TOK_DEV, 0)
        near_mask = key_req[None, :] == query_req[:, None]
        prefix_mask = prefix_group[None, :] == query_grp[:, None]
        all_keys = jnp.concatenate([prefix_keys, near_keys], axis=0)
        all_values = jnp.concatenate([prefix_values, near_values], axis=0)
        all_mask = jnp.concatenate([prefix_mask, near_mask], axis=1)[:, None, :]
        scores = jnp.einsum('thd,khd->thk', query_block, all_keys) * factor
        scores = jnp.where(all_mask, scores, -1e+30)
        largest = lax.optimization_barrier(jnp.max(scores, axis=2, keepdims=True))
        weights = jnp.where(all_mask, jnp.exp(scores - largest), 0.0)
        denominator = lax.optimization_barrier(jnp.sum(weights, axis=2))
        rounded = lax.optimization_barrier(weights.astype(jnp.bfloat16)).astype(jnp.float32)
        summed = jnp.einsum('thk,khd->thd', rounded, all_values)
        return (summed / denominator[:, :, None]).astype(jnp.bfloat16).reshape(TOK_DEV, HEADS * HD)
    attended = lax.map(block, jnp.arange(N_ROW, dtype=jnp.int32)).reshape(TOKENS, HEADS * HD)
    projected = jnp.dot(attended, w_out, preferred_element_type=jnp.float32)
    hidden_out = (hidden_f + gate_rows * projected).astype(jnp.bfloat16)
    return (hidden_out, new_keys.reshape(TOKENS, HEADS * HD), new_values.reshape(TOKENS, HEADS * HD))
```

```python
import functools
import math

import jax
import jax.numpy as jnp
from jax import lax
from jax.experimental import pallas as pl
from jax.experimental.pallas import tpu as pltpu
from jax.sharding import PartitionSpec as P

HD = 128
MOST = 672
KT = 256
HALO = -(-MOST // KT) * KT
MASKED = -1e30
LOWEST = -1e28
ONES = 16
VMEM = 56 * 1024 * 1024


def request_of(positions, req_len):
    starts = jnp.cumsum(req_len) - req_len
    inside = (starts[None, :] <= positions[:, None]).astype(jnp.int32)
    return jnp.sum(inside, axis=1) - 1


def tile_rows(rows, most):
    return max(t for t in range(16, most + 1, 16) if rows % t == 0)


def qkv_kernel(planes, count, z_ref, at_ref, *refs):
    blocks, pieces = refs[:count], refs[count : count + 2 * planes - 1]
    out_ref, a_ref, w_ref, sems = refs[count + 2 * planes - 1 :]
    z = z_ref[0]
    depth = pieces[0].shape[0]
    n, m = blocks[0].shape
    t = pl.program_id(0)

    def each_weight(act):
        for i, piece in enumerate(pieces):
            at = z + i - (planes - 1)

            @pl.when(jnp.logical_and(at >= 0, at < planes))
            def _():
                to = w_ref.at[pl.ds(pl.multiple_of(at * depth, depth), depth), :]
                act(pltpu.make_async_copy(piece, to, sems.at[count + i]))

    def each_block(act, tile):
        for i, block in enumerate(blocks):
            row, column = at_ref[i, 0], at_ref[i, 1]

            @pl.when(row == tile)
            def _():
                to = a_ref.at[pl.ds(pl.multiple_of(row * n, n), n), pl.ds(pl.multiple_of(column * m, m), m)]
                act(pltpu.make_async_copy(block, to, sems.at[i]))

    @pl.when(t == 0)
    def _():
        each_weight(lambda copy: copy.start())
        for tile in range(a_ref.shape[0] // n):
            each_block(lambda copy: copy.start(), tile)
        each_weight(lambda copy: copy.wait())

    each_block(lambda copy: copy.wait(), t)
    a = a_ref[pl.ds(pl.multiple_of(t * n, n), n), :]
    out_ref[...] = jnp.dot(a, w_ref[...], preferred_element_type=jnp.float32).astype(out_ref.dtype)


def qkv_call(z, at, blocks, shape, pieces):
    rows, width = shape
    n, m = blocks[0].shape
    if n % 16 or m % HD:
        whole = jnp.zeros(shape, blocks[0].dtype)
        for i, block in enumerate(blocks):
            whole = lax.dynamic_update_slice(whole, block, (at[i, 0] * n, at[i, 1] * m))
        n, m = shape
        blocks, at = [whole], jnp.zeros((1, 2), jnp.int32)
    planes = (len(pieces) + 1) // 2
    columns = pieces[0].shape[1]
    return pl.pallas_call(
        functools.partial(qkv_kernel, planes, len(blocks)),
        out_shape=jax.ShapeDtypeStruct((rows, columns), jnp.bfloat16),
        grid_spec=pltpu.PrefetchScalarGridSpec(
            num_scalar_prefetch=2,
            grid=(rows // n,),
            in_specs=[pl.BlockSpec(memory_space=pl.ANY)] * (len(blocks) + len(pieces)),
            out_specs=pl.BlockSpec((n, columns), lambda i, *_: (i, 0)),
            scratch_shapes=[
                pltpu.VMEM((rows, width), jnp.bfloat16),
                pltpu.VMEM((width, columns), jnp.bfloat16),
                pltpu.SemaphoreType.DMA((len(blocks) + len(pieces),)),
            ],
        ),
        compiler_params=pltpu.CompilerParams(vmem_limit_bytes=VMEM),
        cost_estimate=pl.CostEstimate(
            flops=2 * rows * width * columns,
            bytes_accessed=2 * (rows * width + width * columns + rows * columns),
            transcendentals=0,
        ),
        name="qkv",
    )(z, at, *blocks, *pieces)


def attention_kernel(heads, groups, need_ref, q_ref, own_ref, low_ref, high_ref, prefix_ref, qtag_ref, ktag_ref,
                     out_ref, kv_ref, vt_ref, m_ref, acc_ref):
    t = pl.program_id(0)
    rows = own_ref.shape[0]
    tiles = ktag_ref.shape[0]
    first = groups * KT
    scale = math.log2(math.e) / math.sqrt(HD)

    @pl.when(t == 0)
    def _():
        for h in range(heads):
            there = slice(h * 2 * HD, (h + 1) * 2 * HD)
            kv_ref[h, first : first + HALO - MOST, :] = jnp.zeros((HALO - MOST, 2 * HD), jnp.bfloat16)
            for g in range(groups):
                kv_ref[h, g * KT : (g + 1) * KT, :] = prefix_ref[g, :, there]
            start = first + HALO
            kv_ref[h, start - MOST : start, :] = low_ref[:, there]
            kv_ref[h, start : start + rows, :] = own_ref[:, h * 3 * HD + HD : (h + 1) * 3 * HD]
            kv_ref[h, start + rows : start + rows + MOST, :] = high_ref[:, there]
            kv_ref[h, start + rows + MOST :, :] = jnp.zeros((HALO - MOST, 2 * HD), jnp.bfloat16)

        def turn(kt, _):
            at = pl.ds(pl.multiple_of(kt * KT, KT), KT)
            for h in range(heads):
                vt_ref[h, kt, :HD, :] = kv_ref[h, at, HD:].T
                vt_ref[h, kt, HD:, :] = jnp.ones((ONES, KT), jnp.bfloat16)
            return 0

        lax.fori_loop(0, tiles, turn, 0)

    m_ref[...] = jnp.full(m_ref.shape, LOWEST, jnp.float32)
    acc_ref[...] = jnp.zeros(acc_ref.shape, jnp.float32)

    def step(kt, _):
        @pl.when(need_ref[t, kt] > 0)
        def _():
            which = (kt >= groups).astype(jnp.int32)
            allowed = ktag_ref[kt] == qtag_ref[which]
            at = pl.ds(pl.multiple_of(kt * KT, KT), KT)
            for h in range(heads):
                q = q_ref[:, h * 3 * HD : h * 3 * HD + HD]
                k = kv_ref[h, at, :HD]
                s = lax.dot_general(k, q, (((1,), (1,)), ((), ())), preferred_element_type=jnp.float32)
                s = jnp.where(allowed, s, MASKED)
                old = m_ref[h]
                new = jnp.maximum(old, jnp.max(s, axis=0, keepdims=True))
                m_ref[h] = new
                p = jnp.exp2(s * scale - new * scale).astype(jnp.bfloat16)
                acc_ref[h] = acc_ref[h] * jnp.exp2((old - new) * scale) + jnp.dot(
                    vt_ref[h, kt], p, preferred_element_type=jnp.float32
                )

        return 0

    lax.fori_loop(0, tiles, step, 0)
    for h in range(heads):
        result = acc_ref[h, :HD] / acc_ref[h, HD : HD + 1]
        out_ref[:, h * HD : (h + 1) * HD] = result.T.astype(out_ref.dtype)


def attention_call(need, qkv, low, high, prefix, qtag, ktag):
    rows = qkv.shape[0]
    heads = qkv.shape[1] // (3 * HD)
    groups = prefix.shape[0]
    tile = rows // need.shape[0]
    tiles = ktag.shape[0]
    whole = lambda shape: pl.BlockSpec(shape, lambda t, *_: (0,) * len(shape))
    return pl.pallas_call(
        functools.partial(attention_kernel, heads, groups),
        out_shape=jax.ShapeDtypeStruct((rows, heads * HD), jnp.bfloat16),
        grid_spec=pltpu.PrefetchScalarGridSpec(
            num_scalar_prefetch=1,
            grid=(rows // tile,),
            in_specs=[
                pl.BlockSpec((tile, heads * 3 * HD), lambda t, *_: (t, 0)),
                whole(qkv.shape),
                whole(low.shape),
                whole(high.shape),
                whole(prefix.shape),
                pl.BlockSpec((2, 1, tile), lambda t, *_: (0, 0, t)),
                whole(ktag.shape),
            ],
            out_specs=pl.BlockSpec((tile, heads * HD), lambda t, *_: (t, 0)),
            scratch_shapes=[
                pltpu.VMEM((heads, tiles * KT, 2 * HD), jnp.bfloat16),
                pltpu.VMEM((heads, tiles, HD + ONES, KT), jnp.bfloat16),
                pltpu.VMEM((heads, 1, tile), jnp.float32),
                pltpu.VMEM((heads, HD + ONES, tile), jnp.float32),
            ],
        ),
        compiler_params=pltpu.CompilerParams(vmem_limit_bytes=VMEM),
        cost_estimate=pl.CostEstimate(
            flops=4 * rows * heads * HD * 8 * KT,
            bytes_accessed=2 * rows * heads * HD * 8,
            transcendentals=rows * heads * 8 * KT,
        ),
        name="attention",
    )(need, qkv, qkv, low, high, prefix, qtag, ktag)


def out_kernel(planes, parts, where_ref, at_ref, hidden_ref, gate_ref, *refs):
    count = 2 * (2 * planes - 1)
    pieces, columns = refs[:count], refs[count : count + parts]
    out_ref, w_ref, a_ref, sems = refs[count + parts :]
    z, x = where_ref[0], where_ref[1]
    depth = pieces[0].shape[0]
    tile = hidden_ref.shape[0]
    t = pl.program_id(0)

    @pl.when(t == 0)
    def _():
        def each(act):
            for i, piece in enumerate(columns):
                m = piece.shape[1]
                to = a_ref.at[:, pl.ds(pl.multiple_of(at_ref[i] * m, m), m)]
                act(pltpu.make_async_copy(piece, to, sems.at[count + i]))
            for i, piece in enumerate(pieces):
                plane = z + i // 2 - (planes - 1)
                at = 2 * plane + (x if i % 2 == 0 else 1 - x)

                @pl.when(jnp.logical_and(plane >= 0, plane < planes))
                def _():
                    to = w_ref.at[pl.ds(pl.multiple_of(at * depth, depth), depth), :]
                    act(pltpu.make_async_copy(piece, to, sems.at[i]))

        each(lambda copy: copy.start())
        each(lambda copy: copy.wait())

    a = a_ref[pl.ds(pl.multiple_of(t * tile, tile), tile), :]
    projected = jnp.dot(a, w_ref[...], preferred_element_type=jnp.float32)
    out_ref[...] = (
        hidden_ref[...].astype(jnp.float32) + gate_ref[...].astype(jnp.float32) * projected
    ).astype(out_ref.dtype)


def out_call(where, at, columns, hidden, gate, pieces):
    rows, width = hidden.shape
    depth = sum(piece.shape[1] for piece in columns)
    planes = (len(pieces) // 2 + 1) // 2
    tile = tile_rows(rows, 256)
    block = pl.BlockSpec((tile, width), lambda i, *_: (i, 0))
    return pl.pallas_call(
        functools.partial(out_kernel, planes, len(columns)),
        out_shape=jax.ShapeDtypeStruct((rows, width), jnp.bfloat16),
        grid_spec=pltpu.PrefetchScalarGridSpec(
            num_scalar_prefetch=2,
            grid=(rows // tile,),
            in_specs=[block, block] + [pl.BlockSpec(memory_space=pl.ANY)] * (len(pieces) + len(columns)),
            out_specs=block,
            scratch_shapes=[
                pltpu.VMEM((depth, width), jnp.bfloat16),
                pltpu.VMEM((rows, depth), jnp.bfloat16),
                pltpu.SemaphoreType.DMA((len(pieces) + len(columns),)),
            ],
        ),
        compiler_params=pltpu.CompilerParams(vmem_limit_bytes=VMEM),
        cost_estimate=pl.CostEstimate(
            flops=2 * rows * width * depth,
            bytes_accessed=2 * (rows * depth + width * depth + 3 * rows * width),
            transcendentals=0,
        ),
        name="project",
    )(where, at, hidden, gate, *pieces, *columns)


def shards(rows_n, cols_n, hidden_in, modulation, w_qkv, w_out, prefix_cache, req_group, req_len, owner):
    planes = rows_n // 2
    tokens, width = hidden_in.shape
    local_heads = w_qkv.shape[1] // (3 * HD)
    heads = local_heads // 2
    parts = 2 if heads % 2 == 0 else 1
    hc = heads // parts
    groups = owner.shape[0]
    requests = req_len.shape[0]
    r, c = lax.axis_index("row"), lax.axis_index("col")
    z, x = r // 2, r % 2
    total = rows_n * tokens

    def swap_x(v, valid=lambda plane: True):
        return lax.ppermute(v, "row", [(i, i ^ 1) for i in range(rows_n) if valid(i // 2)])

    def swap_col(v, bit):
        return lax.ppermute(v, "col", [(i, i ^ bit) for i in range(cols_n)])

    def z_move(v, by, sources):
        pairs = [(2 * p + i, 2 * (p + by) + i) for p in sources for i in range(2)]
        return lax.ppermute(v, "row", pairs)

    under_way = []

    def line_step(v, w, step):
        if len(under_way) >= 2:
            v, w, _, _ = lax.optimization_barrier((v, w) + under_way[-2])
        right = z_move(v, 1, range(step - 1, planes - 1))
        left = z_move(w, -1, range(1, planes - step + 1))
        under_way.append((right, left))
        return right, left

    def line_gather(own):
        lows, highs = [], []
        low = high = own
        for step in range(1, planes):
            low, high = line_step(low, high, step)
            lows.append(low)
            highs.append(high)
        return lows[::-1] + [own] + highs

    def by_x(mine, other, axis):
        return jnp.where(
            x == 0,
            jnp.concatenate([mine, other], axis),
            jnp.concatenate([other, mine], axis),
        )

    def columns_of(v, start, size):
        return lax.dynamic_slice_in_dim(v, start, size, v.ndim - 1)

    def plane_weights(part):
        size = hc * 3 * HD
        mine = columns_of(w_qkv, x * heads * 3 * HD + part * size, size)
        other = columns_of(w_qkv, (1 - x) * heads * 3 * HD + part * size, size)
        return by_x(mine, swap_x(other), 0)

    weights = [plane_weights(part) for part in range(parts)]

    kv_width = heads * 2 * HD
    slot = prefix_cache[0]
    mine = columns_of(slot, x * kv_width, kv_width)
    other = columns_of(slot, (1 - x) * kv_width, kv_width)
    here = by_x(mine[None], swap_x(other)[None], 0)
    owner_plane = owner // 2

    def beyond(plane, side):
        inside = (owner_plane - plane) * side > 0
        return inside, jnp.cumsum(inside.astype(jnp.int32)) - 1

    def outgoing(side, held):
        wanted, order = beyond(z - side, side)
        _, held_order = beyond(z, side)
        source = jnp.where(owner_plane == z, owner % 2, 2 + held_order)
        pool = jnp.concatenate([here, held], 0)
        picked = []
        for j in range(groups - 1):
            at = jnp.sum(jnp.where(wanted & (order == j), source, 0))
            picked.append(lax.dynamic_slice_in_dim(pool, at, 1, 0))
        return jnp.concatenate(picked, 0)

    held_low = held_high = jnp.zeros((groups - 1,) + here.shape[1:], here.dtype)
    for step in range(planes - 1):
        came = z_move(outgoing(-1, held_low), 1, [step])
        held_low = jnp.where(z == step + 1, came, held_low)
        came = z_move(outgoing(1, held_high), -1, [planes - 1 - step])
        held_high = jnp.where(z == planes - 2 - step, came, held_high)
    pool = jnp.concatenate([here, held_low, held_high], 0)
    low_order, high_order = beyond(z, -1)[1], beyond(z, 1)[1]
    source = jnp.where(
        owner_plane == z,
        owner % 2,
        jnp.where(owner_plane < z, 2 + low_order, 2 + groups - 1 + high_order),
    )
    prefix = jnp.concatenate(
        [lax.dynamic_slice_in_dim(pool, source[g], 1, 0) for g in range(groups)], 0
    )

    positions = r * tokens + jnp.arange(tokens, dtype=jnp.int32)
    request_id = request_of(positions, req_len)
    onehot = (request_id[:, None] == jnp.arange(requests, dtype=jnp.int32)[None, :]).astype(jnp.bfloat16)
    shift, scale, gate = [
        jnp.dot(onehot, modulation[:, i, :], preferred_element_type=jnp.float32) for i in range(3)
    ]
    hidden_f = hidden_in.astype(jnp.float32)
    local_mean = jnp.mean(hidden_f, axis=1, keepdims=True)
    local_square = jnp.sum((hidden_f - local_mean) ** 2, axis=1, keepdims=True)
    stats = lax.all_gather(jnp.concatenate([local_mean, local_square], 1).T, "col", axis=0, tiled=False)
    mean = jnp.mean(stats[:, 0], axis=0)
    square = jnp.sum(stats[:, 1], axis=0) + width * jnp.sum((stats[:, 0] - mean[None]) ** 2, axis=0)
    variance = square / (width * cols_n)
    modulated = (
        (hidden_f - mean[:, None]) * lax.rsqrt(variance[:, None] + 1e-06) * (1.0 + scale) + shift
    ).astype(jnp.bfloat16)

    half = tokens // 2
    col_bits = [1 << b for b in reversed(range(cols_n.bit_length() - 1))]
    full_pieces, full_at = [], []
    for i in range(2):
        pieces = [(modulated[i * half : (i + 1) * half], 0, 0)]
        order = [0] + col_bits if i == 0 else col_bits[:-1] + [0] + col_bits[-1:]
        for bit in order:
            if bit == 0:
                pieces += [(swap_x(v), 1, cb) for v, _, cb in pieces]
            else:
                pieces += [(swap_col(v, bit), xb, cb ^ bit) for v, xb, cb in pieces]
        for v, xb, cb in pieces:
            full_pieces.append(v)
            full_at.append(jnp.stack([(x ^ xb) * 2 + i, c ^ cb]))
    full_at = jnp.stack(full_at)

    rows = 2 * tokens
    key_pos = z * rows - HALO + jnp.arange(rows + 2 * HALO, dtype=jnp.int32)
    key_req = request_of(key_pos, req_len)
    key_req = jnp.where(key_pos < 0, -1, jnp.where(key_pos >= total, -2, key_req))
    plane_req = key_req[HALO : HALO + rows]
    plane_group = jnp.sum(
        jnp.where(plane_req[:, None] == jnp.arange(requests, dtype=jnp.int32)[None, :], req_group[None, :], 0), axis=1
    )
    group_tag = jnp.repeat(jnp.arange(groups, dtype=jnp.int32), KT)
    ktag = jnp.concatenate([group_tag, key_req]).reshape(-1, KT, 1)
    qtag = jnp.stack([plane_group, plane_req])[:, None, :]
    tile = tile_rows(rows, 256)
    tile_group = plane_group.reshape(-1, tile)
    tile_req = plane_req.reshape(-1, tile)
    need_group = jnp.any(tile_group[:, None, :] == jnp.arange(groups, dtype=jnp.int32)[None, :, None], axis=2)
    key_tiles = key_req.reshape(-1, KT)
    lowest = jnp.min(jnp.where(key_tiles < 0, requests, key_tiles), axis=1)
    highest = jnp.max(key_tiles, axis=1)
    need_near = (lowest[None, :] <= tile_req[:, -1:]) & (highest[None, :] >= tile_req[:, :1])
    need = jnp.concatenate([need_group, need_near], axis=1).astype(jnp.int32)

    keys = jnp.zeros((tokens, local_heads * HD), jnp.bfloat16)
    values = keys
    attended, attended_at = [], []
    for part in range(parts):
        qkv = qkv_call(z[None], full_at, full_pieces, (rows, width * cols_n), line_gather(weights[part]))

        def kv_of(start, size):
            kv = lax.dynamic_slice_in_dim(qkv, start, size, 0)
            return jnp.concatenate([kv[:, (3 * j + 1) * HD : (3 * j + 3) * HD] for j in range(hc)], 1)

        low = z_move(kv_of(rows - MOST, MOST), 1, range(planes - 1))
        high = z_move(kv_of(0, MOST), -1, range(1, planes))
        own_kv = kv_of(x * tokens, tokens)
        other_kv = swap_x(kv_of((1 - x) * tokens, tokens))
        for xb, v in ((0, own_kv), (1, other_kv)):
            at = ((x ^ xb) * heads + part * hc) * HD
            k = jnp.concatenate([v[:, 2 * j * HD : (2 * j + 1) * HD] for j in range(hc)], 1)
            v = jnp.concatenate([v[:, (2 * j + 1) * HD : (2 * j + 2) * HD] for j in range(hc)], 1)
            keys = lax.dynamic_update_slice(keys, k, (0, at))
            values = lax.dynamic_update_slice(values, v, (0, at))
        part_prefix = prefix[:, :, part * hc * 2 * HD : (part + 1) * hc * 2 * HD]
        out = attention_call(need, qkv, low, high, part_prefix, qtag, ktag)
        pieces = [(lax.dynamic_slice_in_dim(out, x * tokens, tokens, 0), 0, 0)]
        pieces.append((swap_x(lax.dynamic_slice_in_dim(out, (1 - x) * tokens, tokens, 0)), 1, 0))
        for bit in col_bits:
            pieces += [(swap_col(v, bit), xb, cb ^ bit) for v, xb, cb in pieces]
        for v, xb, cb in pieces:
            attended.append(v)
            attended_at.append(((c ^ cb) * 2 + (x ^ xb)) * parts + part)

    out_pieces = []
    for i, piece in enumerate(line_gather(w_out)):
        off = i - (planes - 1)
        out_pieces += [piece, swap_x(piece, lambda p: 0 <= p + off < planes)]
    hidden_out = out_call(
        jnp.stack([z, x]), jnp.stack(attended_at), attended, hidden_in, gate.astype(jnp.bfloat16), out_pieces
    )
    return hidden_out, keys, values


def solution(mesh):
    return jax.shard_map(
        functools.partial(shards, mesh.shape["row"], mesh.shape["col"]),
        mesh=mesh,
        in_specs=(
            P("row", "col"),
            P(None, None, "col"),
            P("row", "col"),
            P("row", "col"),
            P("row", None, "col"),
            P(),
            P(),
            P(),
        ),
        out_specs=(P("row", "col"), P("row", "col"), P("row", "col")),
        check_vma=False,
    )
```

```python
import functools
import math

import jax
import jax.numpy as jnp
from jax import lax
from jax.experimental import pallas as pl
from jax.experimental.pallas import tpu as pltpu
from jax.sharding import PartitionSpec as P

HD = 128
MOST = 672
KT = 256
HALO = -(-MOST // KT) * KT
MASKED = -1e30
LOWEST = -1e28
ONES = 16
VMEM = 56 * 1024 * 1024


def request_of(positions, req_len):
    starts = jnp.cumsum(req_len) - req_len
    inside = (starts[None, :] <= positions[:, None]).astype(jnp.int32)
    return jnp.sum(inside, axis=1) - 1


def tile_rows(rows, most):
    return max(t for t in range(16, most + 1, 16) if rows % t == 0)


def qkv_kernel(planes, count, finish, z_ref, at_ref, *refs):
    blocks = refs[:count]
    pieces = refs[count : -5 if finish else -4]
    start_ref = refs[-5] if finish else None
    out_ref, a_ref, w_ref, sems = refs[-4:]
    z = z_ref[0]
    depth = pieces[0].shape[0]
    n, m = blocks[0].shape
    t = pl.program_id(0)

    def present(plane):
        away = jnp.abs(plane - z)
        return away == planes - 1 if finish else away < planes - 1

    def each_weight(act):
        for i, piece in enumerate(pieces):
            off = (1 - planes, planes - 1)[i] if finish else i - (planes - 2)
            at = z + off

            @pl.when(jnp.logical_and(at >= 0, at < planes))
            def _():
                to = w_ref.at[pl.ds(pl.multiple_of(at * depth, depth), depth), :]
                act(pltpu.make_async_copy(piece, to, sems.at[count + i]))

    def each_block(act, tile):
        for i, block in enumerate(blocks):
            row, column = at_ref[i, 0], at_ref[i, 1]
            used = row == tile
            if finish:
                near = column * m
                first = jnp.logical_and(z == 0, near + m > (planes - 1) * depth)
                used = jnp.logical_and(used, jnp.logical_or(first, jnp.logical_and(z == planes - 1, near < depth)))

            @pl.when(used)
            def _():
                to = a_ref.at[pl.ds(pl.multiple_of(row * n, n), n), pl.ds(pl.multiple_of(column * m, m), m)]
                act(pltpu.make_async_copy(block, to, sems.at[i]))

    @pl.when(t == 0)
    def _():
        each_weight(lambda copy: copy.start())
        for tile in range(a_ref.shape[0] // n):
            each_block(lambda copy: copy.start(), tile)
        each_weight(lambda copy: copy.wait())

    each_block(lambda copy: copy.wait(), t)
    rows = pl.ds(pl.multiple_of(t * n, n), n)

    def product(plane):
        there = slice(plane * depth, (plane + 1) * depth)
        return jnp.dot(a_ref[rows, there], w_ref[there, :], preferred_element_type=jnp.float32)

    if finish:
        out_ref[...] = start_ref[...].astype(out_ref.dtype)
        for plane in (0, planes - 1):

            @pl.when(present(plane))
            def _():
                out_ref[...] = (start_ref[...] + product(plane)).astype(out_ref.dtype)
    else:
        out_ref[...] = jnp.zeros(out_ref.shape, out_ref.dtype)
        for plane in range(planes):

            @pl.when(present(plane))
            def _():
                out_ref[...] += product(plane)


def qkv_call(z, at, blocks, shape, pieces, start=None):
    rows, width = shape
    n, m = blocks[0].shape
    if n % 16 or m % HD:
        whole = jnp.zeros(shape, blocks[0].dtype)
        for i, block in enumerate(blocks):
            whole = lax.dynamic_update_slice(whole, block, (at[i, 0] * n, at[i, 1] * m))
        n, m = shape
        blocks, at = [whole], jnp.zeros((1, 2), jnp.int32)
    finish = start is not None
    depth, columns = pieces[0].shape
    planes = width // depth
    out = pl.BlockSpec((n, columns), lambda i, *_: (i, 0))
    return pl.pallas_call(
        functools.partial(qkv_kernel, planes, len(blocks), finish),
        out_shape=jax.ShapeDtypeStruct((rows, columns), jnp.bfloat16 if finish else jnp.float32),
        grid_spec=pltpu.PrefetchScalarGridSpec(
            num_scalar_prefetch=2,
            grid=(rows // n,),
            in_specs=[pl.BlockSpec(memory_space=pl.ANY)] * (len(blocks) + len(pieces)) + [out] * finish,
            out_specs=out,
            scratch_shapes=[
                pltpu.VMEM((rows, width), jnp.bfloat16),
                pltpu.VMEM((width, columns), jnp.bfloat16),
                pltpu.SemaphoreType.DMA((len(blocks) + len(pieces),)),
            ],
        ),
        compiler_params=pltpu.CompilerParams(vmem_limit_bytes=VMEM),
        cost_estimate=pl.CostEstimate(
            flops=2 * rows * columns * (depth if finish else width),
            bytes_accessed=2 * (rows * width + width * columns + rows * columns),
            transcendentals=0,
        ),
        name="qkv_end" if finish else "qkv_start",
    )(z, at, *blocks, *pieces, *([start] if finish else []))


def attention_kernel(heads, groups, need_ref, q_ref, own_ref, low_ref, high_ref, prefix_ref, qtag_ref, ktag_ref,
                     out_ref, kv_ref, vt_ref, m_ref, acc_ref):
    t = pl.program_id(0)
    rows = own_ref.shape[0]
    tiles = ktag_ref.shape[0]
    first = groups * KT
    scale = math.log2(math.e) / math.sqrt(HD)

    @pl.when(t == 0)
    def _():
        for h in range(heads):
            there = slice(h * 2 * HD, (h + 1) * 2 * HD)
            kv_ref[h, first : first + HALO - MOST, :] = jnp.zeros((HALO - MOST, 2 * HD), jnp.bfloat16)
            for g in range(groups):
                kv_ref[h, g * KT : (g + 1) * KT, :] = prefix_ref[g, :, there]
            start = first + HALO
            kv_ref[h, start - MOST : start, :] = low_ref[:, there]
            kv_ref[h, start : start + rows, :] = own_ref[:, h * 3 * HD + HD : (h + 1) * 3 * HD]
            kv_ref[h, start + rows : start + rows + MOST, :] = high_ref[:, there]
            kv_ref[h, start + rows + MOST :, :] = jnp.zeros((HALO - MOST, 2 * HD), jnp.bfloat16)

        def turn(kt, _):
            at = pl.ds(pl.multiple_of(kt * KT, KT), KT)
            for h in range(heads):
                vt_ref[h, kt, :HD, :] = kv_ref[h, at, HD:].T
                vt_ref[h, kt, HD:, :] = jnp.ones((ONES, KT), jnp.bfloat16)
            return 0

        lax.fori_loop(0, tiles, turn, 0)

    m_ref[...] = jnp.full(m_ref.shape, LOWEST, jnp.float32)
    acc_ref[...] = jnp.zeros(acc_ref.shape, jnp.float32)

    def step(kt, _):
        @pl.when(need_ref[t, kt] > 0)
        def _():
            which = (kt >= groups).astype(jnp.int32)
            allowed = ktag_ref[kt] == qtag_ref[which]
            at = pl.ds(pl.multiple_of(kt * KT, KT), KT)
            for h in range(heads):
                q = q_ref[:, h * 3 * HD : h * 3 * HD + HD]
                k = kv_ref[h, at, :HD]
                s = lax.dot_general(k, q, (((1,), (1,)), ((), ())), preferred_element_type=jnp.float32)
                s = jnp.where(allowed, s, MASKED)
                old = m_ref[h]
                new = jnp.maximum(old, jnp.max(s, axis=0, keepdims=True))
                m_ref[h] = new
                p = jnp.exp2(s * scale - new * scale).astype(jnp.bfloat16)
                acc_ref[h] = acc_ref[h] * jnp.exp2((old - new) * scale) + jnp.dot(
                    vt_ref[h, kt], p, preferred_element_type=jnp.float32
                )

        return 0

    lax.fori_loop(0, tiles, step, 0)
    for h in range(heads):
        result = acc_ref[h, :HD] / acc_ref[h, HD : HD + 1]
        out_ref[:, h * HD : (h + 1) * HD] = result.T.astype(out_ref.dtype)


def attention_call(need, qkv, low, high, prefix, qtag, ktag):
    rows = qkv.shape[0]
    heads = qkv.shape[1] // (3 * HD)
    groups = prefix.shape[0]
    tile = rows // need.shape[0]
    tiles = ktag.shape[0]
    whole = lambda shape: pl.BlockSpec(shape, lambda t, *_: (0,) * len(shape))
    return pl.pallas_call(
        functools.partial(attention_kernel, heads, groups),
        out_shape=jax.ShapeDtypeStruct((rows, heads * HD), jnp.bfloat16),
        grid_spec=pltpu.PrefetchScalarGridSpec(
            num_scalar_prefetch=1,
            grid=(rows // tile,),
            in_specs=[
                pl.BlockSpec((tile, heads * 3 * HD), lambda t, *_: (t, 0)),
                whole(qkv.shape),
                whole(low.shape),
                whole(high.shape),
                whole(prefix.shape),
                pl.BlockSpec((2, 1, tile), lambda t, *_: (0, 0, t)),
                whole(ktag.shape),
            ],
            out_specs=pl.BlockSpec((tile, heads * HD), lambda t, *_: (t, 0)),
            scratch_shapes=[
                pltpu.VMEM((heads, tiles * KT, 2 * HD), jnp.bfloat16),
                pltpu.VMEM((heads, tiles, HD + ONES, KT), jnp.bfloat16),
                pltpu.VMEM((heads, 1, tile), jnp.float32),
                pltpu.VMEM((heads, HD + ONES, tile), jnp.float32),
            ],
        ),
        compiler_params=pltpu.CompilerParams(vmem_limit_bytes=VMEM),
        cost_estimate=pl.CostEstimate(
            flops=4 * rows * heads * HD * 8 * KT,
            bytes_accessed=2 * rows * heads * HD * 8,
            transcendentals=rows * heads * 8 * KT,
        ),
        name="attention",
    )(need, qkv, qkv, low, high, prefix, qtag, ktag)


def out_kernel(planes, parts, where_ref, at_ref, hidden_ref, gate_ref, *refs):
    count = 2 * (2 * planes - 1)
    pieces, columns = refs[:count], refs[count : count + parts]
    out_ref, w_ref, a_ref, sems = refs[count + parts :]
    z, x = where_ref[0], where_ref[1]
    depth = pieces[0].shape[0]
    tile = hidden_ref.shape[0]
    t = pl.program_id(0)

    @pl.when(t == 0)
    def _():
        def each(act):
            for i, piece in enumerate(columns):
                m = piece.shape[1]
                to = a_ref.at[:, pl.ds(pl.multiple_of(at_ref[i] * HD, HD), m)]
                act(pltpu.make_async_copy(piece, to, sems.at[count + i]))
            for i, piece in enumerate(pieces):
                plane = z + i // 2 - (planes - 1)
                at = 2 * plane + (x if i % 2 == 0 else 1 - x)

                @pl.when(jnp.logical_and(plane >= 0, plane < planes))
                def _():
                    to = w_ref.at[pl.ds(pl.multiple_of(at * depth, depth), depth), :]
                    act(pltpu.make_async_copy(piece, to, sems.at[i]))

        each(lambda copy: copy.start())
        each(lambda copy: copy.wait())

    a = a_ref[pl.ds(pl.multiple_of(t * tile, tile), tile), :]
    projected = jnp.dot(a, w_ref[...], preferred_element_type=jnp.float32)
    out_ref[...] = (
        hidden_ref[...].astype(jnp.float32) + gate_ref[...].astype(jnp.float32) * projected
    ).astype(out_ref.dtype)


def out_call(where, at, columns, hidden, gate, pieces):
    rows, width = hidden.shape
    depth = sum(piece.shape[1] for piece in columns)
    planes = (len(pieces) // 2 + 1) // 2
    tile = tile_rows(rows, 256)
    block = pl.BlockSpec((tile, width), lambda i, *_: (i, 0))
    return pl.pallas_call(
        functools.partial(out_kernel, planes, len(columns)),
        out_shape=jax.ShapeDtypeStruct((rows, width), jnp.bfloat16),
        grid_spec=pltpu.PrefetchScalarGridSpec(
            num_scalar_prefetch=2,
            grid=(rows // tile,),
            in_specs=[block, block] + [pl.BlockSpec(memory_space=pl.ANY)] * (len(pieces) + len(columns)),
            out_specs=block,
            scratch_shapes=[
                pltpu.VMEM((depth, width), jnp.bfloat16),
                pltpu.VMEM((rows, depth), jnp.bfloat16),
                pltpu.SemaphoreType.DMA((len(pieces) + len(columns),)),
            ],
        ),
        compiler_params=pltpu.CompilerParams(vmem_limit_bytes=VMEM),
        cost_estimate=pl.CostEstimate(
            flops=2 * rows * width * depth,
            bytes_accessed=2 * (rows * depth + width * depth + 3 * rows * width),
            transcendentals=0,
        ),
        name="project",
    )(where, at, hidden, gate, *pieces, *columns)


def shards(rows_n, cols_n, hidden_in, modulation, w_qkv, w_out, prefix_cache, req_group, req_len, owner):
    planes = rows_n // 2
    tokens, width = hidden_in.shape
    local_heads = w_qkv.shape[1] // (3 * HD)
    heads = local_heads // 2
    counts = [heads // 2] * 2 if heads % 2 == 0 else [heads]
    firsts = [sum(counts[:i]) for i in range(len(counts))]
    parts = len(counts)
    groups = owner.shape[0]
    requests = req_len.shape[0]
    r, c = lax.axis_index("row"), lax.axis_index("col")
    z, x = r // 2, r % 2
    total = rows_n * tokens

    def swap_x(v, valid=lambda plane: True):
        return lax.ppermute(v, "row", [(i, i ^ 1) for i in range(rows_n) if valid(i // 2)])

    def swap_col(v, bit):
        return lax.ppermute(v, "col", [(i, i ^ bit) for i in range(cols_n)])

    def z_move(v, by, sources):
        pairs = [(2 * p + i, 2 * (p + by) + i) for p in sources for i in range(2)]
        return lax.ppermute(v, "row", pairs)

    def after(v, deps):
        return lax.optimization_barrier((v, *deps))[0] if deps else v

    def line_step(v, step, deps=()):
        low, high = lax.optimization_barrier((*v, *deps))[:2] if deps else v
        return (
            z_move(low, 1, range(step - 1, planes - 1)),
            z_move(high, -1, range(1, planes - step + 1)),
        )

    def in_order(own, steps):
        return [low for low, _ in steps[::-1]] + [own] + [high for _, high in steps]

    def by_x(mine, other, axis):
        return jnp.where(
            x == 0,
            jnp.concatenate([mine, other], axis),
            jnp.concatenate([other, mine], axis),
        )

    def columns_of(v, start, size):
        return lax.dynamic_slice_in_dim(v, start, size, v.ndim - 1)

    def plane_weights(part, deps=()):
        size = counts[part] * 3 * HD
        at = firsts[part] * 3 * HD
        mine = columns_of(w_qkv, x * heads * 3 * HD + at, size)
        other = columns_of(w_qkv, (1 - x) * heads * 3 * HD + at, size)
        return by_x(mine, swap_x(after(other, deps)), 0)

    out_steps = [line_step((w_out, w_out), 1)]
    owns = [plane_weights(0)]
    steps = [[line_step((owns[0], owns[0]), 1, out_steps[0])]]
    for part in range(1, parts):
        owns.append(plane_weights(part, owns[:1]))
        steps.append([line_step((owns[part],) * 2, 1)])

    kv_width = heads * 2 * HD
    slot = prefix_cache[0]
    mine = columns_of(slot, x * kv_width, kv_width)
    other = columns_of(slot, (1 - x) * kv_width, kv_width)
    here = by_x(mine[None], swap_x(after(other, owns))[None], 0)
    owner_plane = owner // 2

    def beyond(plane, side):
        inside = (owner_plane - plane) * side > 0
        return inside, jnp.cumsum(inside.astype(jnp.int32)) - 1

    def outgoing(side, held):
        wanted, order = beyond(z - side, side)
        _, held_order = beyond(z, side)
        source = jnp.where(owner_plane == z, owner % 2, 2 + held_order)
        pool = jnp.concatenate([here, held], 0)
        picked = []
        for j in range(groups - 1):
            at = jnp.sum(jnp.where(wanted & (order == j), source, 0))
            picked.append(lax.dynamic_slice_in_dim(pool, at, 1, 0))
        return jnp.concatenate(picked, 0)

    held = [jnp.zeros((groups - 1,) + here.shape[1:], here.dtype)] * 2

    def prefix_step(step, deps):
        last = planes - 1 - step
        low, high = lax.optimization_barrier((outgoing(-1, held[0]), outgoing(1, held[1]), *deps))[:2]
        low, high = z_move(low, 1, [step]), z_move(high, -1, [last])
        held[0] = jnp.where(z == step + 1, low, held[0])
        held[1] = jnp.where(z == last - 1, high, held[1])
        return low, high

    def prefix_of_groups():
        pool = jnp.concatenate([here] + held, 0)
        low_order, high_order = beyond(z, -1)[1], beyond(z, 1)[1]
        source = jnp.where(
            owner_plane == z,
            owner % 2,
            jnp.where(owner_plane < z, 2 + low_order, 2 + groups - 1 + high_order),
        )
        return jnp.concatenate([lax.dynamic_slice_in_dim(pool, source[g], 1, 0) for g in range(groups)], 0)

    positions = r * tokens + jnp.arange(tokens, dtype=jnp.int32)
    request_id = request_of(positions, req_len)
    onehot = (request_id[:, None] == jnp.arange(requests, dtype=jnp.int32)[None, :]).astype(jnp.bfloat16)
    shift, scale, gate = [
        jnp.dot(onehot, modulation[:, i, :], preferred_element_type=jnp.float32) for i in range(3)
    ]
    hidden_f = hidden_in.astype(jnp.float32)
    local_mean = jnp.mean(hidden_f, axis=1, keepdims=True)
    local_square = jnp.sum((hidden_f - local_mean) ** 2, axis=1, keepdims=True)
    stats = lax.all_gather(jnp.concatenate([local_mean, local_square], 1).T, "col", axis=0, tiled=False)
    mean = jnp.mean(stats[:, 0], axis=0)
    square = jnp.sum(stats[:, 1], axis=0) + width * jnp.sum((stats[:, 0] - mean[None]) ** 2, axis=0)
    variance = square / (width * cols_n)
    modulated = (
        (hidden_f - mean[:, None]) * lax.rsqrt(variance[:, None] + 1e-06) * (1.0 + scale) + shift
    ).astype(jnp.bfloat16)

    rows = 2 * tokens
    key_pos = z * rows - HALO + jnp.arange(rows + 2 * HALO, dtype=jnp.int32)
    key_req = request_of(key_pos, req_len)
    key_req = jnp.where(key_pos < 0, -1, jnp.where(key_pos >= total, -2, key_req))
    plane_req = key_req[HALO : HALO + rows]
    plane_group = jnp.sum(
        jnp.where(plane_req[:, None] == jnp.arange(requests, dtype=jnp.int32)[None, :], req_group[None, :], 0), axis=1
    )
    group_tag = jnp.repeat(jnp.arange(groups, dtype=jnp.int32), KT)
    ktag = jnp.concatenate([group_tag, key_req]).reshape(-1, KT, 1)
    qtag = jnp.stack([plane_group, plane_req])[:, None, :]
    tile = tile_rows(rows, 256)
    tile_group = plane_group.reshape(-1, tile)
    tile_req = plane_req.reshape(-1, tile)
    need_group = jnp.any(tile_group[:, None, :] == jnp.arange(groups, dtype=jnp.int32)[None, :, None], axis=2)
    key_tiles = key_req.reshape(-1, KT)
    lowest = jnp.min(jnp.where(key_tiles < 0, requests, key_tiles), axis=1)
    highest = jnp.max(key_tiles, axis=1)
    need_near = (lowest[None, :] <= tile_req[:, -1:]) & (highest[None, :] >= tile_req[:, :1])
    need = jnp.concatenate([need_group, need_near], axis=1).astype(jnp.int32)

    half = tokens // 2
    col_bits = [1 << b for b in reversed(range(cols_n.bit_length() - 1))]
    hops = [[(modulated[i * half : (i + 1) * half], 0, 0)] for i in range(2)]
    orders = [[0] + col_bits, col_bits[:-1] + [0] + col_bits[-1:]]

    def hop(step):
        came = []
        for i in range(2):
            bit = orders[i][step]
            if bit == 0:
                new = [(swap_x(v), 1, cb) for v, _, cb in hops[i]]
            else:
                new = [(swap_col(v, bit), xb, cb ^ bit) for v, xb, cb in hops[i]]
            hops[i] += new
            came += [v for v, _, _ in new]
        return came

    came, hops_left = hop(0) + [need, qtag, ktag], list(range(1, len(col_bits) + 1))
    for step in range(planes - 2):
        for part in range(parts):
            steps[part].append(line_step(steps[part][-1], step + 2, came))
            came = hop(hops_left.pop(0)) if hops_left else ()
        prefix_step(step, steps[-1][step])
    for step in hops_left:
        hop(step)
    prefix_step(planes - 2, steps[-1][-2])
    full_pieces = [v for pieces in hops for v, _, _ in pieces]
    full_at = jnp.stack(
        [jnp.stack([(x ^ xb) * 2 + i, c ^ cb]) for i, pieces in enumerate(hops) for _, xb, cb in pieces]
    )

    def halves(piece, off, deps=()):
        return [piece, swap_x(after(piece, deps), lambda p: 0 <= p + off < planes)]

    first_out = [
        halves(piece, off, steps[-1][-2]) for piece, off in ((out_steps[0][0], -1), (w_out, 0), (out_steps[0][1], 1))
    ]
    begun = [
        qkv_call(z[None], full_at, full_pieces, (rows, width * cols_n), in_order(owns[part], steps[part][:-1]))
        for part in range(parts)
    ]
    keys = jnp.zeros((tokens, local_heads * HD), jnp.bfloat16)
    values = keys
    attended, attended_at = [], []
    for part in range(parts):
        hc = counts[part]
        behind = [v for pair in first_out for v in pair] if part == parts - 1 else []
        qkv = qkv_call(
            after(z[None], behind), full_at, full_pieces, (rows, width * cols_n), steps[part][-1], begun[part]
        )

        def kv_of(start, size):
            kv = lax.dynamic_slice_in_dim(qkv, start, size, 0)
            return jnp.concatenate([kv[:, (3 * j + 1) * HD : (3 * j + 3) * HD] for j in range(hc)], 1)

        low = z_move(kv_of(rows - MOST, MOST), 1, range(planes - 1))
        high = z_move(kv_of(0, MOST), -1, range(1, planes))
        if part == 0:
            for step in range(2, planes):
                out_steps.append(line_step(out_steps[-1], step, (low, high) if step == 2 else ()))
        own_kv = kv_of(x * tokens, tokens)
        other_kv = swap_x(kv_of((1 - x) * tokens, tokens))
        for xb, v in ((0, own_kv), (1, other_kv)):
            at = ((x ^ xb) * heads + firsts[part]) * HD
            k = jnp.concatenate([v[:, 2 * j * HD : (2 * j + 1) * HD] for j in range(hc)], 1)
            v = jnp.concatenate([v[:, (2 * j + 1) * HD : (2 * j + 2) * HD] for j in range(hc)], 1)
            keys = lax.dynamic_update_slice(keys, k, (0, at))
            values = lax.dynamic_update_slice(values, v, (0, at))
        if part == 0:
            prefix = prefix_of_groups()
        part_prefix = prefix[:, :, firsts[part] * 2 * HD : (firsts[part] + hc) * 2 * HD]
        out = attention_call(need, qkv, low, high, part_prefix, qtag, ktag)
        pieces = [(lax.dynamic_slice_in_dim(out, x * tokens, tokens, 0), 0, 0)]
        behind = out_steps[-1] if part == parts - 1 else out_steps[1]
        other = lax.dynamic_slice_in_dim(out, (1 - x) * tokens, tokens, 0)
        pieces.append((swap_x(after(other, behind)), 1, 0))
        for bit in col_bits:
            pieces += [(swap_col(v, bit), xb, cb ^ bit) for v, xb, cb in pieces]
        for v, xb, cb in pieces:
            attended.append(v)
            attended_at.append((c ^ cb) * local_heads + (x ^ xb) * heads + firsts[part])

    out_pairs = first_out
    for step in range(2, planes):
        low, high = out_steps[step - 1]
        out_pairs = [halves(low, -step)] + out_pairs + [halves(high, step)]
    out_pieces = [piece for pair in out_pairs for piece in pair]
    hidden_out = out_call(
        jnp.stack([z, x]), jnp.stack(attended_at), attended, hidden_in, gate.astype(jnp.bfloat16), out_pieces
    )
    return hidden_out, keys, values


def solution(mesh):
    return jax.shard_map(
        functools.partial(shards, mesh.shape["row"], mesh.shape["col"]),
        mesh=mesh,
        in_specs=(
            P("row", "col"),
            P(None, None, "col"),
            P("row", "col"),
            P("row", "col"),
            P("row", None, "col"),
            P(),
            P(),
            P(),
        ),
        out_specs=(P("row", "col"), P("row", "col"), P("row", "col")),
        check_vma=False,
    )
```

```python
import functools
import math

import jax
import jax.numpy as jnp
from jax import lax
from jax.experimental import pallas as pl
from jax.experimental.pallas import tpu as pltpu
from jax.sharding import PartitionSpec as P

HD = 128
MOST = 672
KT = 256
HALO = -(-MOST // KT) * KT
MASKED = -1e30
LOWEST = -1e28
ONES = 16
VMEM = 56 * 1024 * 1024


def request_of(positions, req_len):
    starts = jnp.cumsum(req_len) - req_len
    inside = (starts[None, :] <= positions[:, None]).astype(jnp.int32)
    return jnp.sum(inside, axis=1) - 1


def tile_rows(rows, most):
    return max(t for t in range(16, most + 1, 16) if rows % t == 0)


def qkv_kernel(planes, count, finish, z_ref, at_ref, *refs):
    blocks = refs[:count]
    pieces = refs[count : -5 if finish else -4]
    start_ref = refs[-5] if finish else None
    out_ref, a_ref, w_ref, sems = refs[-4:]
    z = z_ref[0]
    depth = pieces[0].shape[0]
    n, m = blocks[0].shape
    t = pl.program_id(0)

    def present(plane):
        away = jnp.abs(plane - z)
        return away == planes - 1 if finish else away < planes - 1

    def each_weight(act):
        for i, piece in enumerate(pieces):
            off = (1 - planes, planes - 1)[i] if finish else i - (planes - 2)
            at = z + off

            @pl.when(jnp.logical_and(at >= 0, at < planes))
            def _():
                to = w_ref.at[pl.ds(pl.multiple_of(at * depth, depth), depth), :]
                act(pltpu.make_async_copy(piece, to, sems.at[count + i]))

    def each_block(act, tile):
        for i, block in enumerate(blocks):
            row, column = at_ref[i, 0], at_ref[i, 1]
            used = row == tile
            if finish:
                near = column * m
                first = jnp.logical_and(z == 0, near + m > (planes - 1) * depth)
                used = jnp.logical_and(used, jnp.logical_or(first, jnp.logical_and(z == planes - 1, near < depth)))

            @pl.when(used)
            def _():
                to = a_ref.at[pl.ds(pl.multiple_of(row * n, n), n), pl.ds(pl.multiple_of(column * m, m), m)]
                act(pltpu.make_async_copy(block, to, sems.at[i]))

    @pl.when(t == 0)
    def _():
        each_weight(lambda copy: copy.start())
        for tile in range(a_ref.shape[0] // n):
            each_block(lambda copy: copy.start(), tile)
        each_weight(lambda copy: copy.wait())

    each_block(lambda copy: copy.wait(), t)
    rows = pl.ds(pl.multiple_of(t * n, n), n)

    def product(plane):
        there = slice(plane * depth, (plane + 1) * depth)
        return jnp.dot(a_ref[rows, there], w_ref[there, :], preferred_element_type=jnp.float32)

    if finish:
        out_ref[...] = start_ref[...].astype(out_ref.dtype)
        for plane in (0, planes - 1):

            @pl.when(present(plane))
            def _():
                out_ref[...] = (start_ref[...] + product(plane)).astype(out_ref.dtype)
    else:
        out_ref[...] = jnp.zeros(out_ref.shape, out_ref.dtype)
        for plane in range(planes):

            @pl.when(present(plane))
            def _():
                out_ref[...] += product(plane)


def qkv_call(z, at, blocks, shape, pieces, start=None):
    rows, width = shape
    n, m = blocks[0].shape
    if n % 16 or m % HD:
        whole = jnp.zeros(shape, blocks[0].dtype)
        for i, block in enumerate(blocks):
            whole = lax.dynamic_update_slice(whole, block, (at[i, 0] * n, at[i, 1] * m))
        n, m = shape
        blocks, at = [whole], jnp.zeros((1, 2), jnp.int32)
    finish = start is not None
    depth, columns = pieces[0].shape
    planes = width // depth
    out = pl.BlockSpec((n, columns), lambda i, *_: (i, 0))
    return pl.pallas_call(
        functools.partial(qkv_kernel, planes, len(blocks), finish),
        out_shape=jax.ShapeDtypeStruct((rows, columns), jnp.bfloat16 if finish else jnp.float32),
        grid_spec=pltpu.PrefetchScalarGridSpec(
            num_scalar_prefetch=2,
            grid=(rows // n,),
            in_specs=[pl.BlockSpec(memory_space=pl.ANY)] * (len(blocks) + len(pieces)) + [out] * finish,
            out_specs=out,
            scratch_shapes=[
                pltpu.VMEM((rows, width), jnp.bfloat16),
                pltpu.VMEM((width, columns), jnp.bfloat16),
                pltpu.SemaphoreType.DMA((len(blocks) + len(pieces),)),
            ],
        ),
        compiler_params=pltpu.CompilerParams(vmem_limit_bytes=VMEM),
        cost_estimate=pl.CostEstimate(
            flops=2 * rows * columns * (depth if finish else width),
            bytes_accessed=2 * (rows * width + width * columns + rows * columns),
            transcendentals=0,
        ),
        name="qkv_end" if finish else "qkv_start",
    )(z, at, *blocks, *pieces, *([start] if finish else []))


def attention_kernel(heads, groups, need_ref, q_ref, own_ref, low_ref, high_ref, prefix_ref, qtag_ref, ktag_ref,
                     out_ref, kv_ref, vt_ref, m_ref, acc_ref):
    t = pl.program_id(0)
    rows = own_ref.shape[0]
    tiles = ktag_ref.shape[0]
    first = groups * KT
    scale = math.log2(math.e) / math.sqrt(HD)

    @pl.when(t == 0)
    def _():
        for h in range(heads):
            there = slice(h * 2 * HD, (h + 1) * 2 * HD)
            kv_ref[h, first : first + HALO - MOST, :] = jnp.zeros((HALO - MOST, 2 * HD), jnp.bfloat16)
            for g in range(groups):
                kv_ref[h, g * KT : (g + 1) * KT, :] = prefix_ref[g, :, there]
            start = first + HALO
            kv_ref[h, start - MOST : start, :] = low_ref[:, there]
            kv_ref[h, start : start + rows, :] = own_ref[:, h * 3 * HD + HD : (h + 1) * 3 * HD]
            kv_ref[h, start + rows : start + rows + MOST, :] = high_ref[:, there]
            kv_ref[h, start + rows + MOST :, :] = jnp.zeros((HALO - MOST, 2 * HD), jnp.bfloat16)

        def turn(kt, _):
            at = pl.ds(pl.multiple_of(kt * KT, KT), KT)
            for h in range(heads):
                vt_ref[h, kt, :HD, :] = kv_ref[h, at, HD:].T
                vt_ref[h, kt, HD:, :] = jnp.ones((ONES, KT), jnp.bfloat16)
            return 0

        lax.fori_loop(0, tiles, turn, 0)

    m_ref[...] = jnp.full(m_ref.shape, LOWEST, jnp.float32)
    acc_ref[...] = jnp.zeros(acc_ref.shape, jnp.float32)

    def step(kt, _):
        @pl.when(need_ref[t, kt] > 0)
        def _():
            which = (kt >= groups).astype(jnp.int32)
            allowed = ktag_ref[kt] == qtag_ref[which]
            at = pl.ds(pl.multiple_of(kt * KT, KT), KT)
            for h in range(heads):
                q = q_ref[:, h * 3 * HD : h * 3 * HD + HD]
                k = kv_ref[h, at, :HD]
                s = lax.dot_general(k, q, (((1,), (1,)), ((), ())), preferred_element_type=jnp.float32)
                s = jnp.where(allowed, s, MASKED)
                old = m_ref[h]
                new = jnp.maximum(old, jnp.max(s, axis=0, keepdims=True))
                m_ref[h] = new
                p = jnp.exp2(s * scale - new * scale).astype(jnp.bfloat16)
                acc_ref[h] = acc_ref[h] * jnp.exp2((old - new) * scale) + jnp.dot(
                    vt_ref[h, kt], p, preferred_element_type=jnp.float32
                )

        return 0

    lax.fori_loop(0, tiles, step, 0)
    for h in range(heads):
        result = acc_ref[h, :HD] / acc_ref[h, HD : HD + 1]
        out_ref[:, h * HD : (h + 1) * HD] = result.T.astype(out_ref.dtype)


def attention_call(need, qkv, low, high, prefix, qtag, ktag):
    rows = qkv.shape[0]
    heads = qkv.shape[1] // (3 * HD)
    groups = prefix.shape[0]
    tile = rows // need.shape[0]
    tiles = ktag.shape[0]
    whole = lambda shape: pl.BlockSpec(shape, lambda t, *_: (0,) * len(shape))
    return pl.pallas_call(
        functools.partial(attention_kernel, heads, groups),
        out_shape=jax.ShapeDtypeStruct((rows, heads * HD), jnp.bfloat16),
        grid_spec=pltpu.PrefetchScalarGridSpec(
            num_scalar_prefetch=1,
            grid=(rows // tile,),
            in_specs=[
                pl.BlockSpec((tile, heads * 3 * HD), lambda t, *_: (t, 0)),
                whole(qkv.shape),
                whole(low.shape),
                whole(high.shape),
                whole(prefix.shape),
                pl.BlockSpec((2, 1, tile), lambda t, *_: (0, 0, t)),
                whole(ktag.shape),
            ],
            out_specs=pl.BlockSpec((tile, heads * HD), lambda t, *_: (t, 0)),
            scratch_shapes=[
                pltpu.VMEM((heads, tiles * KT, 2 * HD), jnp.bfloat16),
                pltpu.VMEM((heads, tiles, HD + ONES, KT), jnp.bfloat16),
                pltpu.VMEM((heads, 1, tile), jnp.float32),
                pltpu.VMEM((heads, HD + ONES, tile), jnp.float32),
            ],
        ),
        compiler_params=pltpu.CompilerParams(vmem_limit_bytes=VMEM),
        cost_estimate=pl.CostEstimate(
            flops=4 * rows * heads * HD * 8 * KT,
            bytes_accessed=2 * rows * heads * HD * 8,
            transcendentals=rows * heads * 8 * KT,
        ),
        name="attention",
    )(need, qkv, qkv, low, high, prefix, qtag, ktag)


def out_kernel(planes, parts, where_ref, at_ref, hidden_ref, gate_ref, *refs):
    count = 2 * (2 * planes - 1)
    pieces, columns = refs[:count], refs[count : count + parts]
    out_ref, w_ref, a_ref, sems = refs[count + parts :]
    z, x = where_ref[0], where_ref[1]
    depth = pieces[0].shape[0]
    tile = hidden_ref.shape[0]
    t = pl.program_id(0)

    @pl.when(t == 0)
    def _():
        def each(act):
            for i, piece in enumerate(columns):
                m = piece.shape[1]
                to = a_ref.at[:, pl.ds(pl.multiple_of(at_ref[i] * HD, HD), m)]
                act(pltpu.make_async_copy(piece, to, sems.at[count + i]))
            for i, piece in enumerate(pieces):
                plane = z + i // 2 - (planes - 1)
                at = 2 * plane + (x if i % 2 == 0 else 1 - x)

                @pl.when(jnp.logical_and(plane >= 0, plane < planes))
                def _():
                    to = w_ref.at[pl.ds(pl.multiple_of(at * depth, depth), depth), :]
                    act(pltpu.make_async_copy(piece, to, sems.at[i]))

        each(lambda copy: copy.start())
        each(lambda copy: copy.wait())

    a = a_ref[pl.ds(pl.multiple_of(t * tile, tile), tile), :]
    projected = jnp.dot(a, w_ref[...], preferred_element_type=jnp.float32)
    out_ref[...] = (
        hidden_ref[...].astype(jnp.float32) + gate_ref[...].astype(jnp.float32) * projected
    ).astype(out_ref.dtype)


def out_call(where, at, columns, hidden, gate, pieces):
    rows, width = hidden.shape
    depth = sum(piece.shape[1] for piece in columns)
    planes = (len(pieces) // 2 + 1) // 2
    tile = tile_rows(rows, 256)
    block = pl.BlockSpec((tile, width), lambda i, *_: (i, 0))
    return pl.pallas_call(
        functools.partial(out_kernel, planes, len(columns)),
        out_shape=jax.ShapeDtypeStruct((rows, width), jnp.bfloat16),
        grid_spec=pltpu.PrefetchScalarGridSpec(
            num_scalar_prefetch=2,
            grid=(rows // tile,),
            in_specs=[block, block] + [pl.BlockSpec(memory_space=pl.ANY)] * (len(pieces) + len(columns)),
            out_specs=block,
            scratch_shapes=[
                pltpu.VMEM((depth, width), jnp.bfloat16),
                pltpu.VMEM((rows, depth), jnp.bfloat16),
                pltpu.SemaphoreType.DMA((len(pieces) + len(columns),)),
            ],
        ),
        compiler_params=pltpu.CompilerParams(vmem_limit_bytes=VMEM),
        cost_estimate=pl.CostEstimate(
            flops=2 * rows * width * depth,
            bytes_accessed=2 * (rows * depth + width * depth + 3 * rows * width),
            transcendentals=0,
        ),
        name="project",
    )(where, at, hidden, gate, *pieces, *columns)


def shards(rows_n, cols_n, hidden_in, modulation, w_qkv, w_out, prefix_cache, req_group, req_len, owner):
    planes = rows_n // 2
    tokens, width = hidden_in.shape
    local_heads = w_qkv.shape[1] // (3 * HD)
    heads = local_heads // 2
    counts = [heads // 2] * 2 if heads % 2 == 0 else [heads]
    firsts = [sum(counts[:i]) for i in range(len(counts))]
    parts = len(counts)
    groups = owner.shape[0]
    requests = req_len.shape[0]
    r, c = lax.axis_index("row"), lax.axis_index("col")
    z, x = r // 2, r % 2
    total = rows_n * tokens

    def swap_x(v, valid=lambda plane: True):
        return lax.ppermute(v, "row", [(i, i ^ 1) for i in range(rows_n) if valid(i // 2)])

    def swap_col(v, bit):
        return lax.ppermute(v, "col", [(i, i ^ bit) for i in range(cols_n)])

    def z_move(v, by, sources):
        pairs = [(2 * p + i, 2 * (p + by) + i) for p in sources for i in range(2)]
        return lax.ppermute(v, "row", pairs)

    def after(v, deps):
        return lax.optimization_barrier((v, *deps))[0] if deps else v

    def line_step(v, step, deps=()):
        low, high = lax.optimization_barrier((*v, *deps))[:2] if deps else v
        return (
            z_move(low, 1, range(step - 1, planes - 1)),
            z_move(high, -1, range(1, planes - step + 1)),
        )

    def in_order(own, steps):
        return [low for low, _ in steps[::-1]] + [own] + [high for _, high in steps]

    def by_x(mine, other, axis):
        return jnp.where(
            x == 0,
            jnp.concatenate([mine, other], axis),
            jnp.concatenate([other, mine], axis),
        )

    def columns_of(v, start, size):
        return lax.dynamic_slice_in_dim(v, start, size, v.ndim - 1)

    def plane_weights(part, deps=()):
        size = counts[part] * 3 * HD
        at = firsts[part] * 3 * HD
        mine = columns_of(w_qkv, x * heads * 3 * HD + at, size)
        other = columns_of(w_qkv, (1 - x) * heads * 3 * HD + at, size)
        return by_x(mine, swap_x(after(other, deps)), 0)

    out_steps = [line_step((w_out, w_out), 1)]
    owns = [plane_weights(0)]
    steps = [[line_step((owns[0], owns[0]), 1, out_steps[0])]]
    for part in range(1, parts):
        owns.append(plane_weights(part, owns[:1]))
        steps.append([line_step((owns[part],) * 2, 1)])

    kv_width = heads * 2 * HD
    slot = prefix_cache[0]
    mine = columns_of(slot, x * kv_width, kv_width)
    other = columns_of(slot, (1 - x) * kv_width, kv_width)
    here = by_x(mine[None], swap_x(after(other, owns))[None], 0)
    owner_plane = owner // 2

    def beyond(plane, side):
        inside = (owner_plane - plane) * side > 0
        return inside, jnp.cumsum(inside.astype(jnp.int32)) - 1

    def outgoing(side, held):
        wanted, order = beyond(z - side, side)
        _, held_order = beyond(z, side)
        source = jnp.where(owner_plane == z, owner % 2, 2 + held_order)
        pool = jnp.concatenate([here, held], 0)
        picked = []
        for j in range(groups - 1):
            at = jnp.sum(jnp.where(wanted & (order == j), source, 0))
            picked.append(lax.dynamic_slice_in_dim(pool, at, 1, 0))
        return jnp.concatenate(picked, 0)

    held = [jnp.zeros((groups - 1,) + here.shape[1:], here.dtype)] * 2

    def prefix_step(step, deps):
        last = planes - 1 - step
        low, high = lax.optimization_barrier((outgoing(-1, held[0]), outgoing(1, held[1]), *deps))[:2]
        low, high = z_move(low, 1, [step]), z_move(high, -1, [last])
        held[0] = jnp.where(z == step + 1, low, held[0])
        held[1] = jnp.where(z == last - 1, high, held[1])
        return low, high

    def prefix_of_groups():
        pool = jnp.concatenate([here] + held, 0)
        low_order, high_order = beyond(z, -1)[1], beyond(z, 1)[1]
        source = jnp.where(
            owner_plane == z,
            owner % 2,
            jnp.where(owner_plane < z, 2 + low_order, 2 + groups - 1 + high_order),
        )
        return jnp.concatenate([lax.dynamic_slice_in_dim(pool, source[g], 1, 0) for g in range(groups)], 0)

    positions = r * tokens + jnp.arange(tokens, dtype=jnp.int32)
    request_id = request_of(positions, req_len)
    onehot = (request_id[:, None] == jnp.arange(requests, dtype=jnp.int32)[None, :]).astype(jnp.bfloat16)
    shift, scale, gate = [
        jnp.dot(onehot, modulation[:, i, :], preferred_element_type=jnp.float32) for i in range(3)
    ]
    hidden_f = hidden_in.astype(jnp.float32)
    local_mean = jnp.mean(hidden_f, axis=1, keepdims=True)
    local_square = jnp.sum((hidden_f - local_mean) ** 2, axis=1, keepdims=True)
    stats = lax.all_gather(jnp.concatenate([local_mean, local_square], 1).T, "col", axis=0, tiled=False)
    mean = jnp.mean(stats[:, 0], axis=0)
    square = jnp.sum(stats[:, 1], axis=0) + width * jnp.sum((stats[:, 0] - mean[None]) ** 2, axis=0)
    variance = square / (width * cols_n)
    modulated = (
        (hidden_f - mean[:, None]) * lax.rsqrt(variance[:, None] + 1e-06) * (1.0 + scale) + shift
    ).astype(jnp.bfloat16)

    rows = 2 * tokens
    key_pos = z * rows - HALO + jnp.arange(rows + 2 * HALO, dtype=jnp.int32)
    key_req = request_of(key_pos, req_len)
    key_req = jnp.where(key_pos < 0, -1, jnp.where(key_pos >= total, -2, key_req))
    plane_req = key_req[HALO : HALO + rows]
    plane_group = jnp.sum(
        jnp.where(plane_req[:, None] == jnp.arange(requests, dtype=jnp.int32)[None, :], req_group[None, :], 0), axis=1
    )
    group_tag = jnp.repeat(jnp.arange(groups, dtype=jnp.int32), KT)
    ktag = jnp.concatenate([group_tag, key_req]).reshape(-1, KT, 1)
    qtag = jnp.stack([plane_group, plane_req])[:, None, :]
    tile = tile_rows(rows, 256)
    tile_group = plane_group.reshape(-1, tile)
    tile_req = plane_req.reshape(-1, tile)
    need_group = jnp.any(tile_group[:, None, :] == jnp.arange(groups, dtype=jnp.int32)[None, :, None], axis=2)
    key_tiles = key_req.reshape(-1, KT)
    lowest = jnp.min(jnp.where(key_tiles < 0, requests, key_tiles), axis=1)
    highest = jnp.max(key_tiles, axis=1)
    need_near = (lowest[None, :] <= tile_req[:, -1:]) & (highest[None, :] >= tile_req[:, :1])
    need = jnp.concatenate([need_group, need_near], axis=1).astype(jnp.int32)

    half = tokens // 2
    col_bits = [1 << b for b in reversed(range(cols_n.bit_length() - 1))]
    hops = [[(modulated[i * half : (i + 1) * half], 0, 0)] for i in range(2)]
    orders = [[0] + col_bits, col_bits[:-1] + [0] + col_bits[-1:]]

    def hop(step):
        came = []
        for i in range(2):
            bit = orders[i][step]
            if bit == 0:
                new = [(swap_x(v), 1, cb) for v, _, cb in hops[i]]
            else:
                new = [(swap_col(v, bit), xb, cb ^ bit) for v, xb, cb in hops[i]]
            hops[i] += new
            came += [v for v, _, _ in new]
        return came

    came, hops_left = hop(0) + [need, qtag, ktag], list(range(1, len(col_bits) + 1))
    for step in range(planes - 2):
        for part in range(parts):
            steps[part].append(line_step(steps[part][-1], step + 2, came))
            came = hop(hops_left.pop(0)) if hops_left else ()
        prefix_step(step, steps[-1][step])
    for step in hops_left:
        hop(step)
    prefix_step(planes - 2, steps[-1][-2])
    full_pieces = [v for pieces in hops for v, _, _ in pieces]
    full_at = jnp.stack(
        [jnp.stack([(x ^ xb) * 2 + i, c ^ cb]) for i, pieces in enumerate(hops) for _, xb, cb in pieces]
    )

    def halves(piece, off, deps=()):
        return [piece, swap_x(after(piece, deps), lambda p: 0 <= p + off < planes)]

    first_out = [
        halves(piece, off, steps[-1][-2]) for piece, off in ((out_steps[0][0], -1), (w_out, 0), (out_steps[0][1], 1))
    ]
    begun = [
        qkv_call(z[None], full_at, full_pieces, (rows, width * cols_n), in_order(owns[part], steps[part][:-1]))
        for part in range(parts)
    ]
    keys = jnp.zeros((tokens, local_heads * HD), jnp.bfloat16)
    values = keys
    attended, attended_at, later_out = [], [], []
    for part in range(parts):
        hc = counts[part]
        behind = [v for pair in first_out for v in pair] if part == parts - 1 else []
        qkv = qkv_call(
            after(z[None], behind), full_at, full_pieces, (rows, width * cols_n), steps[part][-1], begun[part]
        )

        def kv_of(start, size):
            kv = lax.dynamic_slice_in_dim(qkv, start, size, 0)
            return jnp.concatenate([kv[:, (3 * j + 1) * HD : (3 * j + 3) * HD] for j in range(hc)], 1)

        low = z_move(kv_of(rows - MOST, MOST), 1, range(planes - 1))
        high = z_move(kv_of(0, MOST), -1, range(1, planes))
        if part == 0:
            for step in range(2, planes):
                out_steps.append(line_step(out_steps[-1], step, (low, high) if step == 2 else ()))
                later_out.append([halves(out_steps[-1][0], -step), halves(out_steps[-1][1], step)])
        own_kv = kv_of(x * tokens, tokens)
        other_kv = swap_x(kv_of((1 - x) * tokens, tokens))
        for xb, v in ((0, own_kv), (1, other_kv)):
            at = ((x ^ xb) * heads + firsts[part]) * HD
            k = jnp.concatenate([v[:, 2 * j * HD : (2 * j + 1) * HD] for j in range(hc)], 1)
            v = jnp.concatenate([v[:, (2 * j + 1) * HD : (2 * j + 2) * HD] for j in range(hc)], 1)
            keys = lax.dynamic_update_slice(keys, k, (0, at))
            values = lax.dynamic_update_slice(values, v, (0, at))
        if part == 0:
            prefix = prefix_of_groups()
        part_prefix = prefix[:, :, firsts[part] * 2 * HD : (firsts[part] + hc) * 2 * HD]
        out = attention_call(need, qkv, low, high, part_prefix, qtag, ktag)
        pieces = [(lax.dynamic_slice_in_dim(out, x * tokens, tokens, 0), 0, 0)]
        behind = out_steps[1]
        if part == parts - 1:
            behind = [*out_steps[-1], *(piece for pairs in later_out[:-1] for _, piece in pairs)]
        other = lax.dynamic_slice_in_dim(out, (1 - x) * tokens, tokens, 0)
        pieces.append((swap_x(after(other, behind)), 1, 0))
        for bit in col_bits:
            pieces += [(swap_col(v, bit), xb, cb ^ bit) for v, xb, cb in pieces]
        for v, xb, cb in pieces:
            attended.append(v)
            attended_at.append((c ^ cb) * local_heads + (x ^ xb) * heads + firsts[part])

    out_pairs = first_out
    for low, high in later_out:
        out_pairs = [low] + out_pairs + [high]
    out_pieces = [piece for pair in out_pairs for piece in pair]
    hidden_out = out_call(
        jnp.stack([z, x]), jnp.stack(attended_at), attended, hidden_in, gate.astype(jnp.bfloat16), out_pieces
    )
    return hidden_out, keys, values


def solution(mesh):
    return jax.shard_map(
        functools.partial(shards, mesh.shape["row"], mesh.shape["col"]),
        mesh=mesh,
        in_specs=(
            P("row", "col"),
            P(None, None, "col"),
            P("row", "col"),
            P("row", "col"),
            P("row", None, "col"),
            P(),
            P(),
            P(),
        ),
        out_specs=(P("row", "col"), P("row", "col"), P("row", "col")),
        check_vma=False,
    )
```

```python
import functools
import math

import jax
import jax.numpy as jnp
from jax import lax
from jax.experimental import pallas as pl
from jax.experimental.pallas import tpu as pltpu
from jax.sharding import PartitionSpec as P

HD = 128
MOST = 672
KT = 256
HALO = -(-MOST // KT) * KT
MASKED = -1e30
LOWEST = -1e28
ONES = 16
VMEM = 56 * 1024 * 1024


def request_of(positions, req_len):
    starts = jnp.cumsum(req_len) - req_len
    inside = (starts[None, :] <= positions[:, None]).astype(jnp.int32)
    return jnp.sum(inside, axis=1) - 1


def tile_rows(rows, most):
    return max(t for t in range(16, most + 1, 16) if rows % t == 0)


def qkv_kernel(planes, count, finish, z_ref, at_ref, *refs):
    blocks = refs[:count]
    pieces = refs[count : -5 if finish else -4]
    start_ref = refs[-5] if finish else None
    out_ref, a_ref, w_ref, sems = refs[-4:]
    z = z_ref[0]
    depth = pieces[0].shape[0]
    n, m = blocks[0].shape
    t = pl.program_id(0)

    def present(plane):
        away = jnp.abs(plane - z)
        return away == planes - 1 if finish else away < planes - 1

    def each_weight(act):
        for i, piece in enumerate(pieces):
            off = (1 - planes, planes - 1)[i] if finish else i - (planes - 2)
            at = z + off

            @pl.when(jnp.logical_and(at >= 0, at < planes))
            def _():
                to = w_ref.at[pl.ds(pl.multiple_of(at * depth, depth), depth), :]
                act(pltpu.make_async_copy(piece, to, sems.at[count + i]))

    def each_block(act, tile):
        for i, block in enumerate(blocks):
            row, column = at_ref[i, 0], at_ref[i, 1]
            used = row == tile
            if finish:
                near = column * m
                first = jnp.logical_and(z == 0, near + m > (planes - 1) * depth)
                used = jnp.logical_and(used, jnp.logical_or(first, jnp.logical_and(z == planes - 1, near < depth)))

            @pl.when(used)
            def _():
                to = a_ref.at[pl.ds(pl.multiple_of(row * n, n), n), pl.ds(pl.multiple_of(column * m, m), m)]
                act(pltpu.make_async_copy(block, to, sems.at[i]))

    @pl.when(t == 0)
    def _():
        each_weight(lambda copy: copy.start())
        for tile in range(a_ref.shape[0] // n):
            each_block(lambda copy: copy.start(), tile)
        each_weight(lambda copy: copy.wait())

    each_block(lambda copy: copy.wait(), t)
    rows = pl.ds(pl.multiple_of(t * n, n), n)

    def product(plane):
        there = slice(plane * depth, (plane + 1) * depth)
        return jnp.dot(a_ref[rows, there], w_ref[there, :], preferred_element_type=jnp.float32)

    if finish:
        out_ref[...] = start_ref[...].astype(out_ref.dtype)
        for plane in (0, planes - 1):

            @pl.when(present(plane))
            def _():
                out_ref[...] = (start_ref[...] + product(plane)).astype(out_ref.dtype)
    else:
        out_ref[...] = jnp.zeros(out_ref.shape, out_ref.dtype)
        for plane in range(planes):

            @pl.when(present(plane))
            def _():
                out_ref[...] += product(plane)


def qkv_call(z, at, blocks, shape, pieces, start=None):
    rows, width = shape
    n, m = blocks[0].shape
    if n % 16 or m % HD:
        whole = jnp.zeros(shape, blocks[0].dtype)
        for i, block in enumerate(blocks):
            whole = lax.dynamic_update_slice(whole, block, (at[i, 0] * n, at[i, 1] * m))
        n, m = shape
        blocks, at = [whole], jnp.zeros((1, 2), jnp.int32)
    finish = start is not None
    depth, columns = pieces[0].shape
    planes = width // depth
    out = pl.BlockSpec((n, columns), lambda i, *_: (i, 0))
    return pl.pallas_call(
        functools.partial(qkv_kernel, planes, len(blocks), finish),
        out_shape=jax.ShapeDtypeStruct((rows, columns), jnp.bfloat16 if finish else jnp.float32),
        grid_spec=pltpu.PrefetchScalarGridSpec(
            num_scalar_prefetch=2,
            grid=(rows // n,),
            in_specs=[pl.BlockSpec(memory_space=pl.ANY)] * (len(blocks) + len(pieces)) + [out] * finish,
            out_specs=out,
            scratch_shapes=[
                pltpu.VMEM((rows, width), jnp.bfloat16),
                pltpu.VMEM((width, columns), jnp.bfloat16),
                pltpu.SemaphoreType.DMA((len(blocks) + len(pieces),)),
            ],
        ),
        compiler_params=pltpu.CompilerParams(vmem_limit_bytes=VMEM),
        cost_estimate=pl.CostEstimate(
            flops=2 * rows * columns * (depth if finish else width),
            bytes_accessed=2 * (rows * width + width * columns + rows * columns),
            transcendentals=0,
        ),
        name="qkv_end" if finish else "qkv_start",
    )(z, at, *blocks, *pieces, *([start] if finish else []))


def attention_kernel(heads, groups, need_ref, q_ref, own_ref, low_ref, high_ref, prefix_ref, qtag_ref, ktag_ref,
                     out_ref, kv_ref, vt_ref, m_ref, acc_ref):
    t = pl.program_id(0)
    rows = own_ref.shape[0]
    tiles = ktag_ref.shape[0]
    first = groups * KT
    scale = math.log2(math.e) / math.sqrt(HD)

    @pl.when(t == 0)
    def _():
        for h in range(heads):
            there = slice(h * 2 * HD, (h + 1) * 2 * HD)
            kv_ref[h, first : first + HALO - MOST, :] = jnp.zeros((HALO - MOST, 2 * HD), jnp.bfloat16)
            for g in range(groups):
                kv_ref[h, g * KT : (g + 1) * KT, :] = prefix_ref[g, :, there]
            start = first + HALO
            kv_ref[h, start - MOST : start, :] = low_ref[:, there]
            kv_ref[h, start : start + rows, :] = own_ref[:, h * 3 * HD + HD : (h + 1) * 3 * HD]
            kv_ref[h, start + rows : start + rows + MOST, :] = high_ref[:, there]
            kv_ref[h, start + rows + MOST :, :] = jnp.zeros((HALO - MOST, 2 * HD), jnp.bfloat16)

        def turn(kt, _):
            at = pl.ds(pl.multiple_of(kt * KT, KT), KT)
            for h in range(heads):
                vt_ref[h, kt, :HD, :] = kv_ref[h, at, HD:].T
                vt_ref[h, kt, HD:, :] = jnp.ones((ONES, KT), jnp.bfloat16)
            return 0

        lax.fori_loop(0, tiles, turn, 0)

    m_ref[...] = jnp.full(m_ref.shape, LOWEST, jnp.float32)
    acc_ref[...] = jnp.zeros(acc_ref.shape, jnp.float32)

    def step(kt, _):
        @pl.when(need_ref[t, kt] > 0)
        def _():
            which = (kt >= groups).astype(jnp.int32)
            allowed = ktag_ref[kt] == qtag_ref[which]
            at = pl.ds(pl.multiple_of(kt * KT, KT), KT)
            for h in range(heads):
                q = q_ref[:, h * 3 * HD : h * 3 * HD + HD]
                k = kv_ref[h, at, :HD]
                s = lax.dot_general(k, q, (((1,), (1,)), ((), ())), preferred_element_type=jnp.float32)
                s = jnp.where(allowed, s, MASKED)
                old = m_ref[h]
                new = jnp.maximum(old, jnp.max(s, axis=0, keepdims=True))
                m_ref[h] = new
                p = jnp.exp2(s * scale - new * scale).astype(jnp.bfloat16)
                acc_ref[h] = acc_ref[h] * jnp.exp2((old - new) * scale) + jnp.dot(
                    vt_ref[h, kt], p, preferred_element_type=jnp.float32
                )

        return 0

    lax.fori_loop(0, tiles, step, 0)
    for h in range(heads):
        result = acc_ref[h, :HD] / acc_ref[h, HD : HD + 1]
        out_ref[:, h * HD : (h + 1) * HD] = result.T.astype(out_ref.dtype)


def attention_call(need, qkv, low, high, prefix, qtag, ktag):
    rows = qkv.shape[0]
    heads = qkv.shape[1] // (3 * HD)
    groups = prefix.shape[0]
    tile = rows // need.shape[0]
    tiles = ktag.shape[0]
    whole = lambda shape: pl.BlockSpec(shape, lambda t, *_: (0,) * len(shape))
    return pl.pallas_call(
        functools.partial(attention_kernel, heads, groups),
        out_shape=jax.ShapeDtypeStruct((rows, heads * HD), jnp.bfloat16),
        grid_spec=pltpu.PrefetchScalarGridSpec(
            num_scalar_prefetch=1,
            grid=(rows // tile,),
            in_specs=[
                pl.BlockSpec((tile, heads * 3 * HD), lambda t, *_: (t, 0)),
                whole(qkv.shape),
                whole(low.shape),
                whole(high.shape),
                whole(prefix.shape),
                pl.BlockSpec((2, 1, tile), lambda t, *_: (0, 0, t)),
                whole(ktag.shape),
            ],
            out_specs=pl.BlockSpec((tile, heads * HD), lambda t, *_: (t, 0)),
            scratch_shapes=[
                pltpu.VMEM((heads, tiles * KT, 2 * HD), jnp.bfloat16),
                pltpu.VMEM((heads, tiles, HD + ONES, KT), jnp.bfloat16),
                pltpu.VMEM((heads, 1, tile), jnp.float32),
                pltpu.VMEM((heads, HD + ONES, tile), jnp.float32),
            ],
        ),
        compiler_params=pltpu.CompilerParams(vmem_limit_bytes=VMEM),
        cost_estimate=pl.CostEstimate(
            flops=4 * rows * heads * HD * 8 * KT,
            bytes_accessed=2 * rows * heads * HD * 8,
            transcendentals=rows * heads * 8 * KT,
        ),
        name="attention",
    )(need, qkv, qkv, low, high, prefix, qtag, ktag)


def out_kernel(planes, parts, where_ref, at_ref, hidden_ref, gate_ref, *refs):
    count = 2 * (2 * planes - 1)
    pieces, columns = refs[:count], refs[count : count + parts]
    out_ref, w_ref, a_ref, sems = refs[count + parts :]
    z, x = where_ref[0], where_ref[1]
    depth = pieces[0].shape[0]
    tile = hidden_ref.shape[0]
    t = pl.program_id(0)

    @pl.when(t == 0)
    def _():
        def each(act):
            for i, piece in enumerate(columns):
                m = piece.shape[1]
                to = a_ref.at[:, pl.ds(pl.multiple_of(at_ref[i] * HD, HD), m)]
                act(pltpu.make_async_copy(piece, to, sems.at[count + i]))
            for i, piece in enumerate(pieces):
                plane = z + i // 2 - (planes - 1)
                at = 2 * plane + (x if i % 2 == 0 else 1 - x)

                @pl.when(jnp.logical_and(plane >= 0, plane < planes))
                def _():
                    to = w_ref.at[pl.ds(pl.multiple_of(at * depth, depth), depth), :]
                    act(pltpu.make_async_copy(piece, to, sems.at[i]))

        each(lambda copy: copy.start())
        each(lambda copy: copy.wait())

    a = a_ref[pl.ds(pl.multiple_of(t * tile, tile), tile), :]
    projected = jnp.dot(a, w_ref[...], preferred_element_type=jnp.float32)
    out_ref[...] = (
        hidden_ref[...].astype(jnp.float32) + gate_ref[...].astype(jnp.float32) * projected
    ).astype(out_ref.dtype)


def out_call(where, at, columns, hidden, gate, pieces):
    rows, width = hidden.shape
    depth = sum(piece.shape[1] for piece in columns)
    planes = (len(pieces) // 2 + 1) // 2
    tile = tile_rows(rows, 256)
    block = pl.BlockSpec((tile, width), lambda i, *_: (i, 0))
    return pl.pallas_call(
        functools.partial(out_kernel, planes, len(columns)),
        out_shape=jax.ShapeDtypeStruct((rows, width), jnp.bfloat16),
        grid_spec=pltpu.PrefetchScalarGridSpec(
            num_scalar_prefetch=2,
            grid=(rows // tile,),
            in_specs=[block, block] + [pl.BlockSpec(memory_space=pl.ANY)] * (len(pieces) + len(columns)),
            out_specs=block,
            scratch_shapes=[
                pltpu.VMEM((depth, width), jnp.bfloat16),
                pltpu.VMEM((rows, depth), jnp.bfloat16),
                pltpu.SemaphoreType.DMA((len(pieces) + len(columns),)),
            ],
        ),
        compiler_params=pltpu.CompilerParams(vmem_limit_bytes=VMEM),
        cost_estimate=pl.CostEstimate(
            flops=2 * rows * width * depth,
            bytes_accessed=2 * (rows * depth + width * depth + 3 * rows * width),
            transcendentals=0,
        ),
        name="project",
    )(where, at, hidden, gate, *pieces, *columns)


def shards(rows_n, cols_n, hidden_in, modulation, w_qkv, w_out, prefix_cache, req_group, req_len, owner):
    planes = rows_n // 2
    tokens, width = hidden_in.shape
    local_heads = w_qkv.shape[1] // (3 * HD)
    heads = local_heads // 2
    counts = [heads // 2] * 2 if heads % 2 == 0 else [heads]
    firsts = [sum(counts[:i]) for i in range(len(counts))]
    parts = len(counts)
    groups = owner.shape[0]
    requests = req_len.shape[0]
    r, c = lax.axis_index("row"), lax.axis_index("col")
    z, x = r // 2, r % 2
    total = rows_n * tokens

    def swap_x(v, valid=lambda plane: True):
        return lax.ppermute(v, "row", [(i, i ^ 1) for i in range(rows_n) if valid(i // 2)])

    def swap_col(v, bit):
        return lax.ppermute(v, "col", [(i, i ^ bit) for i in range(cols_n)])

    def z_move(v, by, sources):
        pairs = [(2 * p + i, 2 * (p + by) + i) for p in sources for i in range(2)]
        return lax.ppermute(v, "row", pairs)

    def after(v, deps):
        return lax.optimization_barrier((v, *deps))[0] if deps else v

    def line_step(v, step, deps=()):
        low, high = lax.optimization_barrier((*v, *deps))[:2] if deps else v
        return (
            z_move(low, 1, range(step - 1, planes - 1)),
            z_move(high, -1, range(1, planes - step + 1)),
        )

    def in_order(own, steps):
        return [low for low, _ in steps[::-1]] + [own] + [high for _, high in steps]

    def by_x(mine, other, axis):
        return jnp.where(
            x == 0,
            jnp.concatenate([mine, other], axis),
            jnp.concatenate([other, mine], axis),
        )

    def columns_of(v, start, size):
        return lax.dynamic_slice_in_dim(v, start, size, v.ndim - 1)

    def plane_weights(part, deps=()):
        size = counts[part] * 3 * HD
        at = firsts[part] * 3 * HD
        mine = columns_of(w_qkv, x * heads * 3 * HD + at, size)
        other = columns_of(w_qkv, (1 - x) * heads * 3 * HD + at, size)
        return by_x(mine, swap_x(after(other, deps)), 0)

    out_steps = [line_step((w_out, w_out), 1)]
    owns = [plane_weights(0)]
    steps = [[line_step((owns[0], owns[0]), 1, out_steps[0])]]
    for part in range(1, parts):
        owns.append(plane_weights(part, owns[:1]))
        steps.append([line_step((owns[part],) * 2, 1)])

    kv_width = heads * 2 * HD
    slot = prefix_cache[0]
    mine = columns_of(slot, x * kv_width, kv_width)
    other = columns_of(slot, (1 - x) * kv_width, kv_width)
    here = by_x(mine[None], swap_x(after(other, owns))[None], 0)
    owner_plane = owner // 2

    def beyond(plane, side):
        inside = (owner_plane - plane) * side > 0
        return inside, jnp.cumsum(inside.astype(jnp.int32)) - 1

    def outgoing(side, held):
        wanted, order = beyond(z - side, side)
        _, held_order = beyond(z, side)
        source = jnp.where(owner_plane == z, owner % 2, 2 + held_order)
        pool = jnp.concatenate([here, held], 0)
        picked = []
        for j in range(groups - 1):
            at = jnp.sum(jnp.where(wanted & (order == j), source, 0))
            picked.append(lax.dynamic_slice_in_dim(pool, at, 1, 0))
        return jnp.concatenate(picked, 0)

    held = [jnp.zeros((groups - 1,) + here.shape[1:], here.dtype)] * 2

    def prefix_step(step, deps):
        last = planes - 1 - step
        low, high = lax.optimization_barrier((outgoing(-1, held[0]), outgoing(1, held[1]), *deps))[:2]
        low, high = z_move(low, 1, [step]), z_move(high, -1, [last])
        held[0] = jnp.where(z == step + 1, low, held[0])
        held[1] = jnp.where(z == last - 1, high, held[1])
        return low, high

    def prefix_of_groups():
        pool = jnp.concatenate([here] + held, 0)
        low_order, high_order = beyond(z, -1)[1], beyond(z, 1)[1]
        source = jnp.where(
            owner_plane == z,
            owner % 2,
            jnp.where(owner_plane < z, 2 + low_order, 2 + groups - 1 + high_order),
        )
        return jnp.concatenate([lax.dynamic_slice_in_dim(pool, source[g], 1, 0) for g in range(groups)], 0)

    positions = r * tokens + jnp.arange(tokens, dtype=jnp.int32)
    request_id = request_of(positions, req_len)
    onehot = (request_id[:, None] == jnp.arange(requests, dtype=jnp.int32)[None, :]).astype(jnp.bfloat16)
    shift, scale, gate = [
        jnp.dot(onehot, modulation[:, i, :], preferred_element_type=jnp.float32) for i in range(3)
    ]
    hidden_f = hidden_in.astype(jnp.float32)
    local_mean = jnp.mean(hidden_f, axis=1, keepdims=True)
    local_square = jnp.sum((hidden_f - local_mean) ** 2, axis=1, keepdims=True)
    stats = lax.all_gather(jnp.concatenate([local_mean, local_square], 1).T, "col", axis=0, tiled=False)
    mean = jnp.mean(stats[:, 0], axis=0)
    square = jnp.sum(stats[:, 1], axis=0) + width * jnp.sum((stats[:, 0] - mean[None]) ** 2, axis=0)
    variance = square / (width * cols_n)
    modulated = (
        (hidden_f - mean[:, None]) * lax.rsqrt(variance[:, None] + 1e-06) * (1.0 + scale) + shift
    ).astype(jnp.bfloat16)

    rows = 2 * tokens
    key_pos = z * rows - HALO + jnp.arange(rows + 2 * HALO, dtype=jnp.int32)
    key_req = request_of(key_pos, req_len)
    key_req = jnp.where(key_pos < 0, -1, jnp.where(key_pos >= total, -2, key_req))
    plane_req = key_req[HALO : HALO + rows]
    plane_group = jnp.sum(
        jnp.where(plane_req[:, None] == jnp.arange(requests, dtype=jnp.int32)[None, :], req_group[None, :], 0), axis=1
    )
    group_tag = jnp.repeat(jnp.arange(groups, dtype=jnp.int32), KT)
    ktag = jnp.concatenate([group_tag, key_req]).reshape(-1, KT, 1)
    qtag = jnp.stack([plane_group, plane_req])[:, None, :]
    tile = tile_rows(rows, 256)
    tile_group = plane_group.reshape(-1, tile)
    tile_req = plane_req.reshape(-1, tile)
    need_group = jnp.any(tile_group[:, None, :] == jnp.arange(groups, dtype=jnp.int32)[None, :, None], axis=2)
    key_tiles = key_req.reshape(-1, KT)
    lowest = jnp.min(jnp.where(key_tiles < 0, requests, key_tiles), axis=1)
    highest = jnp.max(key_tiles, axis=1)
    need_near = (lowest[None, :] <= tile_req[:, -1:]) & (highest[None, :] >= tile_req[:, :1])
    need = jnp.concatenate([need_group, need_near], axis=1).astype(jnp.int32)

    half = tokens // 2
    col_bits = [1 << b for b in reversed(range(cols_n.bit_length() - 1))]
    hops = [[(modulated[i * half : (i + 1) * half], 0, 0)] for i in range(2)]
    orders = [[0] + col_bits, col_bits[:-1] + [0] + col_bits[-1:]]

    def hop(step):
        came = []
        for i in range(2):
            bit = orders[i][step]
            if bit == 0:
                new = [(swap_x(v), 1, cb) for v, _, cb in hops[i]]
            else:
                new = [(swap_col(v, bit), xb, cb ^ bit) for v, xb, cb in hops[i]]
            hops[i] += new
            came += [v for v, _, _ in new]
        return came

    came, hops_left = hop(0) + [need, qtag, ktag], list(range(1, len(col_bits) + 1))
    for step in range(planes - 2):
        for part in range(parts):
            steps[part].append(line_step(steps[part][-1], step + 2, came))
            came = hop(hops_left.pop(0)) if hops_left else ()
        prefix_step(step, steps[-1][step])
    for step in hops_left:
        hop(step)
    prefix_step(planes - 2, steps[-1][-2])
    full_pieces = [v for pieces in hops for v, _, _ in pieces]
    full_at = jnp.stack(
        [jnp.stack([(x ^ xb) * 2 + i, c ^ cb]) for i, pieces in enumerate(hops) for _, xb, cb in pieces]
    )

    def halves(piece, off, deps=()):
        return [piece, swap_x(after(piece, deps), lambda p: 0 <= p + off < planes)]

    first_out = [
        halves(piece, off, steps[-1][-2]) for piece, off in ((out_steps[0][0], -1), (w_out, 0), (out_steps[0][1], 1))
    ]
    begun = [
        qkv_call(z[None], full_at, full_pieces, (rows, width * cols_n), in_order(owns[part], steps[part][:-1]))
        for part in range(parts)
    ]
    keys = jnp.zeros((tokens, local_heads * HD), jnp.bfloat16)
    values = keys
    attended, attended_at, later_out = [], [], []
    for part in range(parts):
        hc = counts[part]
        behind = [v for pair in first_out for v in pair] if part == parts - 1 else []
        qkv = qkv_call(
            after(z[None], behind), full_at, full_pieces, (rows, width * cols_n), steps[part][-1], begun[part]
        )

        def kv_of(start, size):
            kv = lax.dynamic_slice_in_dim(qkv, start, size, 0)
            return jnp.concatenate([kv[:, (3 * j + 1) * HD : (3 * j + 3) * HD] for j in range(hc)], 1)

        low = z_move(kv_of(rows - MOST, MOST), 1, range(planes - 1))
        high = z_move(kv_of(0, MOST), -1, range(1, planes))
        if part == 0:
            out_steps.append(line_step(out_steps[-1], 2, (low, high)))
        own_kv = kv_of(x * tokens, tokens)
        other_kv = swap_x(kv_of((1 - x) * tokens, tokens))
        for xb, v in ((0, own_kv), (1, other_kv)):
            at = ((x ^ xb) * heads + firsts[part]) * HD
            k = jnp.concatenate([v[:, 2 * j * HD : (2 * j + 1) * HD] for j in range(hc)], 1)
            v = jnp.concatenate([v[:, (2 * j + 1) * HD : (2 * j + 2) * HD] for j in range(hc)], 1)
            keys = lax.dynamic_update_slice(keys, k, (0, at))
            values = lax.dynamic_update_slice(values, v, (0, at))
        if part == 0:
            prefix = prefix_of_groups()
        part_prefix = prefix[:, :, firsts[part] * 2 * HD : (firsts[part] + hc) * 2 * HD]
        out = attention_call(need, qkv, low, high, part_prefix, qtag, ktag)
        if part == 0:
            for step in range(2, planes):
                if step > 2:
                    out_steps.append(line_step(out_steps[-1], step, [out]))
                later_out.append([halves(out_steps[-1][0], -step, [out]), halves(out_steps[-1][1], step, [out])])
        pieces = [(lax.dynamic_slice_in_dim(out, x * tokens, tokens, 0), 0, 0)]
        behind = out_steps[1]
        if part == parts - 1:
            behind = [*out_steps[-1], *(piece for pairs in later_out[:-1] for _, piece in pairs)]
        other = lax.dynamic_slice_in_dim(out, (1 - x) * tokens, tokens, 0)
        pieces.append((swap_x(after(other, behind)), 1, 0))
        for bit in col_bits:
            pieces += [(swap_col(v, bit), xb, cb ^ bit) for v, xb, cb in pieces]
        for v, xb, cb in pieces:
            attended.append(v)
            attended_at.append((c ^ cb) * local_heads + (x ^ xb) * heads + firsts[part])

    out_pairs = first_out
    for low, high in later_out:
        out_pairs = [low] + out_pairs + [high]
    out_pieces = [piece for pair in out_pairs for piece in pair]
    hidden_out = out_call(
        jnp.stack([z, x]), jnp.stack(attended_at), attended, hidden_in, gate.astype(jnp.bfloat16), out_pieces
    )
    return hidden_out, keys, values


def solution(mesh):
    return jax.shard_map(
        functools.partial(shards, mesh.shape["row"], mesh.shape["col"]),
        mesh=mesh,
        in_specs=(
            P("row", "col"),
            P(None, None, "col"),
            P("row", "col"),
            P("row", "col"),
            P("row", None, "col"),
            P(),
            P(),
            P(),
        ),
        out_specs=(P("row", "col"), P("row", "col"), P("row", "col")),
        check_vma=False,
    )
```

```python
import functools
import math

import jax
import jax.numpy as jnp
from jax import lax
from jax.experimental import pallas as pl
from jax.experimental.pallas import tpu as pltpu
from jax.sharding import PartitionSpec as P

HD = 128
MOST = 672
KT = 256
HALO = -(-MOST // KT) * KT
MASKED = -1e30
LOWEST = -1e28
ONES = 16
VMEM = 56 * 1024 * 1024


def request_of(positions, req_len):
    starts = jnp.cumsum(req_len) - req_len
    inside = (starts[None, :] <= positions[:, None]).astype(jnp.int32)
    return jnp.sum(inside, axis=1) - 1


def tile_rows(rows, most):
    return max(t for t in range(16, most + 1, 16) if rows % t == 0)


def qkv_kernel(planes, count, finish, z_ref, at_ref, *refs):
    blocks = refs[:count]
    pieces = refs[count : -5 if finish else -4]
    start_ref = refs[-5] if finish else None
    out_ref, a_ref, w_ref, sems = refs[-4:]
    z = z_ref[0]
    depth = pieces[0].shape[0]
    n, m = blocks[0].shape
    t = pl.program_id(0)

    def present(plane):
        away = jnp.abs(plane - z)
        return away == planes - 1 if finish else away < planes - 1

    def each_weight(act):
        for i, piece in enumerate(pieces):
            off = (1 - planes, planes - 1)[i] if finish else i - (planes - 2)
            at = z + off

            @pl.when(jnp.logical_and(at >= 0, at < planes))
            def _():
                to = w_ref.at[pl.ds(pl.multiple_of(at * depth, depth), depth), :]
                act(pltpu.make_async_copy(piece, to, sems.at[count + i]))

    def each_block(act, tile):
        for i, block in enumerate(blocks):
            row, column = at_ref[i, 0], at_ref[i, 1]
            used = row == tile
            if finish:
                near = column * m
                first = jnp.logical_and(z == 0, near + m > (planes - 1) * depth)
                used = jnp.logical_and(used, jnp.logical_or(first, jnp.logical_and(z == planes - 1, near < depth)))

            @pl.when(used)
            def _():
                to = a_ref.at[pl.ds(pl.multiple_of(row * n, n), n), pl.ds(pl.multiple_of(column * m, m), m)]
                act(pltpu.make_async_copy(block, to, sems.at[i]))

    @pl.when(t == 0)
    def _():
        each_weight(lambda copy: copy.start())
        for tile in range(a_ref.shape[0] // n):
            each_block(lambda copy: copy.start(), tile)
        each_weight(lambda copy: copy.wait())

    each_block(lambda copy: copy.wait(), t)
    rows = pl.ds(pl.multiple_of(t * n, n), n)

    def product(plane):
        there = slice(plane * depth, (plane + 1) * depth)
        return jnp.dot(a_ref[rows, there], w_ref[there, :], preferred_element_type=jnp.float32)

    if finish:
        out_ref[...] = start_ref[...].astype(out_ref.dtype)
        for plane in (0, planes - 1):

            @pl.when(present(plane))
            def _():
                out_ref[...] = (start_ref[...] + product(plane)).astype(out_ref.dtype)
    else:
        out_ref[...] = jnp.zeros(out_ref.shape, out_ref.dtype)
        for plane in range(planes):

            @pl.when(present(plane))
            def _():
                out_ref[...] += product(plane)


def qkv_call(z, at, blocks, shape, pieces, start=None):
    rows, width = shape
    n, m = blocks[0].shape
    if n % 16 or m % HD:
        whole = jnp.zeros(shape, blocks[0].dtype)
        for i, block in enumerate(blocks):
            whole = lax.dynamic_update_slice(whole, block, (at[i, 0] * n, at[i, 1] * m))
        n, m = shape
        blocks, at = [whole], jnp.zeros((1, 2), jnp.int32)
    finish = start is not None
    depth, columns = pieces[0].shape
    planes = width // depth
    out = pl.BlockSpec((n, columns), lambda i, *_: (i, 0))
    return pl.pallas_call(
        functools.partial(qkv_kernel, planes, len(blocks), finish),
        out_shape=jax.ShapeDtypeStruct((rows, columns), jnp.bfloat16 if finish else jnp.float32),
        grid_spec=pltpu.PrefetchScalarGridSpec(
            num_scalar_prefetch=2,
            grid=(rows // n,),
            in_specs=[pl.BlockSpec(memory_space=pl.ANY)] * (len(blocks) + len(pieces)) + [out] * finish,
            out_specs=out,
            scratch_shapes=[
                pltpu.VMEM((rows, width), jnp.bfloat16),
                pltpu.VMEM((width, columns), jnp.bfloat16),
                pltpu.SemaphoreType.DMA((len(blocks) + len(pieces),)),
            ],
        ),
        compiler_params=pltpu.CompilerParams(vmem_limit_bytes=VMEM),
        cost_estimate=pl.CostEstimate(
            flops=2 * rows * columns * (depth if finish else width),
            bytes_accessed=2 * (rows * width + width * columns + rows * columns),
            transcendentals=0,
        ),
        name="qkv_end" if finish else "qkv_start",
    )(z, at, *blocks, *pieces, *([start] if finish else []))


def attention_kernel(heads, groups, need_ref, q_ref, own_ref, low_ref, high_ref, prefix_ref, qtag_ref, ktag_ref,
                     out_ref, kv_ref, vt_ref, m_ref, acc_ref):
    t = pl.program_id(0)
    rows = own_ref.shape[0]
    tiles = ktag_ref.shape[0]
    first = groups * KT
    scale = math.log2(math.e) / math.sqrt(HD)

    @pl.when(t == 0)
    def _():
        for h in range(heads):
            there = slice(h * 2 * HD, (h + 1) * 2 * HD)
            kv_ref[h, first : first + HALO - MOST, :] = jnp.zeros((HALO - MOST, 2 * HD), jnp.bfloat16)
            for g in range(groups):
                kv_ref[h, g * KT : (g + 1) * KT, :] = prefix_ref[g, :, there]
            start = first + HALO
            kv_ref[h, start - MOST : start, :] = low_ref[:, there]
            kv_ref[h, start : start + rows, :] = own_ref[:, h * 3 * HD + HD : (h + 1) * 3 * HD]
            kv_ref[h, start + rows : start + rows + MOST, :] = high_ref[:, there]
            kv_ref[h, start + rows + MOST :, :] = jnp.zeros((HALO - MOST, 2 * HD), jnp.bfloat16)

        def turn(kt, _):
            at = pl.ds(pl.multiple_of(kt * KT, KT), KT)
            for h in range(heads):
                vt_ref[h, kt, :HD, :] = kv_ref[h, at, HD:].T
                vt_ref[h, kt, HD:, :] = jnp.ones((ONES, KT), jnp.bfloat16)
            return 0

        lax.fori_loop(0, tiles, turn, 0)

    m_ref[...] = jnp.full(m_ref.shape, LOWEST, jnp.float32)
    acc_ref[...] = jnp.zeros(acc_ref.shape, jnp.float32)

    def step(kt, _):
        @pl.when(need_ref[t, kt] > 0)
        def _():
            which = (kt >= groups).astype(jnp.int32)
            allowed = ktag_ref[kt] == qtag_ref[which]
            at = pl.ds(pl.multiple_of(kt * KT, KT), KT)
            for h in range(heads):
                q = q_ref[:, h * 3 * HD : h * 3 * HD + HD]
                k = kv_ref[h, at, :HD]
                s = lax.dot_general(k, q, (((1,), (1,)), ((), ())), preferred_element_type=jnp.float32)
                s = jnp.where(allowed, s, MASKED)
                old = m_ref[h]
                new = jnp.maximum(old, jnp.max(s, axis=0, keepdims=True))
                m_ref[h] = new
                p = jnp.exp2(s * scale - new * scale).astype(jnp.bfloat16)
                acc_ref[h] = acc_ref[h] * jnp.exp2((old - new) * scale) + jnp.dot(
                    vt_ref[h, kt], p, preferred_element_type=jnp.float32
                )

        return 0

    lax.fori_loop(0, tiles, step, 0)
    for h in range(heads):
        result = acc_ref[h, :HD] / acc_ref[h, HD : HD + 1]
        out_ref[:, h * HD : (h + 1) * HD] = result.T.astype(out_ref.dtype)


def attention_call(need, qkv, low, high, prefix, qtag, ktag):
    rows = qkv.shape[0]
    heads = qkv.shape[1] // (3 * HD)
    groups = prefix.shape[0]
    tile = rows // need.shape[0]
    tiles = ktag.shape[0]
    whole = lambda shape: pl.BlockSpec(shape, lambda t, *_: (0,) * len(shape))
    return pl.pallas_call(
        functools.partial(attention_kernel, heads, groups),
        out_shape=jax.ShapeDtypeStruct((rows, heads * HD), jnp.bfloat16),
        grid_spec=pltpu.PrefetchScalarGridSpec(
            num_scalar_prefetch=1,
            grid=(rows // tile,),
            in_specs=[
                pl.BlockSpec((tile, heads * 3 * HD), lambda t, *_: (t, 0)),
                whole(qkv.shape),
                whole(low.shape),
                whole(high.shape),
                whole(prefix.shape),
                pl.BlockSpec((2, 1, tile), lambda t, *_: (0, 0, t)),
                whole(ktag.shape),
            ],
            out_specs=pl.BlockSpec((tile, heads * HD), lambda t, *_: (t, 0)),
            scratch_shapes=[
                pltpu.VMEM((heads, tiles * KT, 2 * HD), jnp.bfloat16),
                pltpu.VMEM((heads, tiles, HD + ONES, KT), jnp.bfloat16),
                pltpu.VMEM((heads, 1, tile), jnp.float32),
                pltpu.VMEM((heads, HD + ONES, tile), jnp.float32),
            ],
        ),
        compiler_params=pltpu.CompilerParams(vmem_limit_bytes=VMEM),
        cost_estimate=pl.CostEstimate(
            flops=4 * rows * heads * HD * 8 * KT,
            bytes_accessed=2 * rows * heads * HD * 8,
            transcendentals=rows * heads * 8 * KT,
        ),
        name="attention",
    )(need, qkv, qkv, low, high, prefix, qtag, ktag)


def out_kernel(planes, parts, where_ref, at_ref, hidden_ref, gate_ref, *refs):
    count = 2 * (2 * planes - 1)
    pieces, columns = refs[:count], refs[count : count + parts]
    out_ref, w_ref, a_ref, sems = refs[count + parts :]
    z, x = where_ref[0], where_ref[1]
    depth = pieces[0].shape[0]
    tile = hidden_ref.shape[0]
    t = pl.program_id(0)

    @pl.when(t == 0)
    def _():
        def each(act):
            for i, piece in enumerate(columns):
                m = piece.shape[1]
                to = a_ref.at[:, pl.ds(pl.multiple_of(at_ref[i] * HD, HD), m)]
                act(pltpu.make_async_copy(piece, to, sems.at[count + i]))
            for i, piece in enumerate(pieces):
                plane = z + i // 2 - (planes - 1)
                at = 2 * plane + (x if i % 2 == 0 else 1 - x)

                @pl.when(jnp.logical_and(plane >= 0, plane < planes))
                def _():
                    to = w_ref.at[pl.ds(pl.multiple_of(at * depth, depth), depth), :]
                    act(pltpu.make_async_copy(piece, to, sems.at[i]))

        each(lambda copy: copy.start())
        each(lambda copy: copy.wait())

    a = a_ref[pl.ds(pl.multiple_of(t * tile, tile), tile), :]
    projected = jnp.dot(a, w_ref[...], preferred_element_type=jnp.float32)
    out_ref[...] = (
        hidden_ref[...].astype(jnp.float32) + gate_ref[...].astype(jnp.float32) * projected
    ).astype(out_ref.dtype)


def out_call(where, at, columns, hidden, gate, pieces):
    rows, width = hidden.shape
    depth = sum(piece.shape[1] for piece in columns)
    planes = (len(pieces) // 2 + 1) // 2
    tile = tile_rows(rows, 256)
    block = pl.BlockSpec((tile, width), lambda i, *_: (i, 0))
    return pl.pallas_call(
        functools.partial(out_kernel, planes, len(columns)),
        out_shape=jax.ShapeDtypeStruct((rows, width), jnp.bfloat16),
        grid_spec=pltpu.PrefetchScalarGridSpec(
            num_scalar_prefetch=2,
            grid=(rows // tile,),
            in_specs=[block, block] + [pl.BlockSpec(memory_space=pl.ANY)] * (len(pieces) + len(columns)),
            out_specs=block,
            scratch_shapes=[
                pltpu.VMEM((depth, width), jnp.bfloat16),
                pltpu.VMEM((rows, depth), jnp.bfloat16),
                pltpu.SemaphoreType.DMA((len(pieces) + len(columns),)),
            ],
        ),
        compiler_params=pltpu.CompilerParams(vmem_limit_bytes=VMEM),
        cost_estimate=pl.CostEstimate(
            flops=2 * rows * width * depth,
            bytes_accessed=2 * (rows * depth + width * depth + 3 * rows * width),
            transcendentals=0,
        ),
        name="project",
    )(where, at, hidden, gate, *pieces, *columns)


def shards(rows_n, cols_n, hidden_in, modulation, w_qkv, w_out, prefix_cache, req_group, req_len, owner):
    planes = rows_n // 2
    tokens, width = hidden_in.shape
    local_heads = w_qkv.shape[1] // (3 * HD)
    heads = local_heads // 2
    counts = [heads // 2] * 2 if heads % 2 == 0 else [heads]
    firsts = [sum(counts[:i]) for i in range(len(counts))]
    parts = len(counts)
    groups = owner.shape[0]
    requests = req_len.shape[0]
    r, c = lax.axis_index("row"), lax.axis_index("col")
    z, x = r // 2, r % 2
    total = rows_n * tokens

    def swap_x(v, valid=lambda plane: True):
        return lax.ppermute(v, "row", [(i, i ^ 1) for i in range(rows_n) if valid(i // 2)])

    def swap_col(v, bit):
        return lax.ppermute(v, "col", [(i, i ^ bit) for i in range(cols_n)])

    def z_move(v, by, sources):
        pairs = [(2 * p + i, 2 * (p + by) + i) for p in sources for i in range(2)]
        return lax.ppermute(v, "row", pairs)

    def after(v, deps):
        return lax.optimization_barrier((v, *deps))[0] if deps else v

    def line_step(v, step, deps=()):
        low, high = lax.optimization_barrier((*v, *deps))[:2] if deps else v
        return (
            z_move(low, 1, range(step - 1, planes - 1)),
            z_move(high, -1, range(1, planes - step + 1)),
        )

    def in_order(own, steps):
        return [low for low, _ in steps[::-1]] + [own] + [high for _, high in steps]

    def by_x(mine, other, axis):
        return jnp.where(
            x == 0,
            jnp.concatenate([mine, other], axis),
            jnp.concatenate([other, mine], axis),
        )

    def columns_of(v, start, size):
        return lax.dynamic_slice_in_dim(v, start, size, v.ndim - 1)

    def plane_weights(part, deps=()):
        size = counts[part] * 3 * HD
        at = firsts[part] * 3 * HD
        mine = columns_of(w_qkv, x * heads * 3 * HD + at, size)
        other = columns_of(w_qkv, (1 - x) * heads * 3 * HD + at, size)
        return by_x(mine, swap_x(after(other, deps)), 0)

    out_steps = [line_step((w_out, w_out), 1)]
    owns = [plane_weights(0)]
    steps = [[line_step((owns[0], owns[0]), 1, out_steps[0])]]
    for part in range(1, parts):
        owns.append(plane_weights(part, owns[:1]))
        steps.append([line_step((owns[part],) * 2, 1)])

    kv_width = heads * 2 * HD
    slot = prefix_cache[0]
    mine = columns_of(slot, x * kv_width, kv_width)
    other = columns_of(slot, (1 - x) * kv_width, kv_width)
    here = by_x(mine[None], swap_x(after(other, owns))[None], 0)
    owner_plane = owner // 2

    def beyond(plane, side):
        inside = (owner_plane - plane) * side > 0
        return inside, jnp.cumsum(inside.astype(jnp.int32)) - 1

    def outgoing(side, held):
        wanted, order = beyond(z - side, side)
        _, held_order = beyond(z, side)
        source = jnp.where(owner_plane == z, owner % 2, 2 + held_order)
        pool = jnp.concatenate([here, held], 0)
        picked = []
        for j in range(groups - 1):
            at = jnp.sum(jnp.where(wanted & (order == j), source, 0))
            picked.append(lax.dynamic_slice_in_dim(pool, at, 1, 0))
        return jnp.concatenate(picked, 0)

    held = [jnp.zeros((groups - 1,) + here.shape[1:], here.dtype)] * 2

    def prefix_step(step, deps):
        last = planes - 1 - step
        low, high = lax.optimization_barrier((outgoing(-1, held[0]), outgoing(1, held[1]), *deps))[:2]
        low, high = z_move(low, 1, [step]), z_move(high, -1, [last])
        held[0] = jnp.where(z == step + 1, low, held[0])
        held[1] = jnp.where(z == last - 1, high, held[1])
        return low, high

    def prefix_of_groups():
        pool = jnp.concatenate([here] + held, 0)
        low_order, high_order = beyond(z, -1)[1], beyond(z, 1)[1]
        source = jnp.where(
            owner_plane == z,
            owner % 2,
            jnp.where(owner_plane < z, 2 + low_order, 2 + groups - 1 + high_order),
        )
        return jnp.concatenate([lax.dynamic_slice_in_dim(pool, source[g], 1, 0) for g in range(groups)], 0)

    positions = r * tokens + jnp.arange(tokens, dtype=jnp.int32)
    request_id = request_of(positions, req_len)
    onehot = (request_id[:, None] == jnp.arange(requests, dtype=jnp.int32)[None, :]).astype(jnp.bfloat16)
    shift, scale, gate = [
        jnp.dot(onehot, modulation[:, i, :], preferred_element_type=jnp.float32) for i in range(3)
    ]
    hidden_f = hidden_in.astype(jnp.float32)
    local_mean = jnp.mean(hidden_f, axis=1, keepdims=True)
    local_square = jnp.sum((hidden_f - local_mean) ** 2, axis=1, keepdims=True)
    stats = lax.all_gather(jnp.concatenate([local_mean, local_square], 1).T, "col", axis=0, tiled=False)
    mean = jnp.mean(stats[:, 0], axis=0)
    square = jnp.sum(stats[:, 1], axis=0) + width * jnp.sum((stats[:, 0] - mean[None]) ** 2, axis=0)
    variance = square / (width * cols_n)
    modulated = (
        (hidden_f - mean[:, None]) * lax.rsqrt(variance[:, None] + 1e-06) * (1.0 + scale) + shift
    ).astype(jnp.bfloat16)

    rows = 2 * tokens
    key_pos = z * rows - HALO + jnp.arange(rows + 2 * HALO, dtype=jnp.int32)
    key_req = request_of(key_pos, req_len)
    key_req = jnp.where(key_pos < 0, -1, jnp.where(key_pos >= total, -2, key_req))
    plane_req = key_req[HALO : HALO + rows]
    plane_group = jnp.sum(
        jnp.where(plane_req[:, None] == jnp.arange(requests, dtype=jnp.int32)[None, :], req_group[None, :], 0), axis=1
    )
    group_tag = jnp.repeat(jnp.arange(groups, dtype=jnp.int32), KT)
    ktag = jnp.concatenate([group_tag, key_req]).reshape(-1, KT, 1)
    qtag = jnp.stack([plane_group, plane_req])[:, None, :]
    tile = tile_rows(rows, 512)
    tile_group = plane_group.reshape(-1, tile)
    tile_req = plane_req.reshape(-1, tile)
    need_group = jnp.any(tile_group[:, None, :] == jnp.arange(groups, dtype=jnp.int32)[None, :, None], axis=2)
    key_tiles = key_req.reshape(-1, KT)
    lowest = jnp.min(jnp.where(key_tiles < 0, requests, key_tiles), axis=1)
    highest = jnp.max(key_tiles, axis=1)
    need_near = (lowest[None, :] <= tile_req[:, -1:]) & (highest[None, :] >= tile_req[:, :1])
    need = jnp.concatenate([need_group, need_near], axis=1).astype(jnp.int32)

    half = tokens // 2
    col_bits = [1 << b for b in reversed(range(cols_n.bit_length() - 1))]
    hops = [[(modulated[i * half : (i + 1) * half], 0, 0)] for i in range(2)]
    orders = [[0] + col_bits, col_bits[:-1] + [0] + col_bits[-1:]]

    def hop(step):
        came = []
        for i in range(2):
            bit = orders[i][step]
            if bit == 0:
                new = [(swap_x(v), 1, cb) for v, _, cb in hops[i]]
            else:
                new = [(swap_col(v, bit), xb, cb ^ bit) for v, xb, cb in hops[i]]
            hops[i] += new
            came += [v for v, _, _ in new]
        return came

    came, hops_left = hop(0) + [need, qtag, ktag], list(range(1, len(col_bits) + 1))
    for step in range(planes - 2):
        for part in range(parts):
            steps[part].append(line_step(steps[part][-1], step + 2, came))
            came = hop(hops_left.pop(0)) if hops_left else ()
        prefix_step(step, steps[-1][step])
    for step in hops_left:
        hop(step)
    prefix_step(planes - 2, steps[-1][-2])
    full_pieces = [v for pieces in hops for v, _, _ in pieces]
    full_at = jnp.stack(
        [jnp.stack([(x ^ xb) * 2 + i, c ^ cb]) for i, pieces in enumerate(hops) for _, xb, cb in pieces]
    )

    def halves(piece, off, deps=()):
        return [piece, swap_x(after(piece, deps), lambda p: 0 <= p + off < planes)]

    first_out = [
        halves(piece, off, steps[-1][-2]) for piece, off in ((out_steps[0][0], -1), (w_out, 0), (out_steps[0][1], 1))
    ]
    begun = [
        qkv_call(z[None], full_at, full_pieces, (rows, width * cols_n), in_order(owns[part], steps[part][:-1]))
        for part in range(parts)
    ]
    keys = jnp.zeros((tokens, local_heads * HD), jnp.bfloat16)
    values = keys
    attended, attended_at, later_out = [], [], []
    for part in range(parts):
        hc = counts[part]
        behind = [v for pair in first_out for v in pair] if part == parts - 1 else []
        qkv = qkv_call(
            after(z[None], behind), full_at, full_pieces, (rows, width * cols_n), steps[part][-1], begun[part]
        )

        def kv_of(start, size):
            kv = lax.dynamic_slice_in_dim(qkv, start, size, 0)
            return jnp.concatenate([kv[:, (3 * j + 1) * HD : (3 * j + 3) * HD] for j in range(hc)], 1)

        low = z_move(kv_of(rows - MOST, MOST), 1, range(planes - 1))
        high = z_move(kv_of(0, MOST), -1, range(1, planes))
        if part == 0:
            for step in range(2, planes):
                out_steps.append(line_step(out_steps[-1], step, (low, high) if step == 2 else ()))
                later_out.append([halves(out_steps[-1][0], -step), halves(out_steps[-1][1], step)])
        own_kv = kv_of(x * tokens, tokens)
        other_kv = swap_x(kv_of((1 - x) * tokens, tokens))
        for xb, v in ((0, own_kv), (1, other_kv)):
            at = ((x ^ xb) * heads + firsts[part]) * HD
            k = jnp.concatenate([v[:, 2 * j * HD : (2 * j + 1) * HD] for j in range(hc)], 1)
            v = jnp.concatenate([v[:, (2 * j + 1) * HD : (2 * j + 2) * HD] for j in range(hc)], 1)
            keys = lax.dynamic_update_slice(keys, k, (0, at))
            values = lax.dynamic_update_slice(values, v, (0, at))
        if part == 0:
            prefix = prefix_of_groups()
        part_prefix = prefix[:, :, firsts[part] * 2 * HD : (firsts[part] + hc) * 2 * HD]
        out = attention_call(need, qkv, low, high, part_prefix, qtag, ktag)
        pieces = [(lax.dynamic_slice_in_dim(out, x * tokens, tokens, 0), 0, 0)]
        behind = out_steps[1]
        if part == parts - 1:
            behind = [*out_steps[-1], *(piece for pairs in later_out[:-1] for _, piece in pairs)]
        other = lax.dynamic_slice_in_dim(out, (1 - x) * tokens, tokens, 0)
        pieces.append((swap_x(after(other, behind)), 1, 0))
        for bit in col_bits:
            pieces += [(swap_col(v, bit), xb, cb ^ bit) for v, xb, cb in pieces]
        for v, xb, cb in pieces:
            attended.append(v)
            attended_at.append((c ^ cb) * local_heads + (x ^ xb) * heads + firsts[part])

    out_pairs = first_out
    for low, high in later_out:
        out_pairs = [low] + out_pairs + [high]
    out_pieces = [piece for pair in out_pairs for piece in pair]
    hidden_out = out_call(
        jnp.stack([z, x]), jnp.stack(attended_at), attended, hidden_in, gate.astype(jnp.bfloat16), out_pieces
    )
    return hidden_out, keys, values


def solution(mesh):
    return jax.shard_map(
        functools.partial(shards, mesh.shape["row"], mesh.shape["col"]),
        mesh=mesh,
        in_specs=(
            P("row", "col"),
            P(None, None, "col"),
            P("row", "col"),
            P("row", "col"),
            P("row", None, "col"),
            P(),
            P(),
            P(),
        ),
        out_specs=(P("row", "col"), P("row", "col"), P("row", "col")),
        check_vma=False,
    )
```
